256 devices in a mesh: dp: 8 (over z), expert: 32 (over x, y, core).
Axes of the slice: x: 4, y: 4, z: 8, core: 2. Of those that a mesh axis runs over, the one named last changes fastest.
Arguments:
- queries: bfloat16 [256, 2560], replicated, may hold values from -8 to 8
- patch_keys: bfloat16 [131072, 2560], P(('dp', 'expert')), may hold values from -160 to 160
- patch_values: bfloat16 [131072, 2560], P(('dp', 'expert')), may hold values from -6 to 6
- norm_gain: float32 [2560], replicated, may hold values from 0.25 to 1.75
- gate_weight: bfloat16 [32, 2560, 832], P('expert', 'dp'), may hold values from -0.125 to 0.125
- up_weight: bfloat16 [32, 2560, 832], P('expert', 'dp'), may hold values from -0.125 to 0.125
- down_weight: bfloat16 [32, 832, 2560], P('expert', None, 'dp'), may hold values from -0.21875 to 0.21875
- expert_ids: int32 [32768, 6], P(('dp', 'expert')), may hold values from 0 to 31, all different within a row; in each aligned block of 128 rows (0 to 127, 128 to 255, ...) at most 28 rows name the same one
- combine_weights: float32 [32768, 6], P(('dp', 'expert')), may hold values from 0.1 to 1
- latent_grad: bfloat16 [32768, 2560], P(('dp', 'expert')), may hold values from -6 to 6
Outputs:
- layer_out: bfloat16 [32768, 2560], P(('dp', 'expert'))
- query_grad: float32 [256, 2560], replicated
The draws below stay inside these ranges and needn't reach their ends.
Inputs may be any that keep to these rules, and one draw needn't show every extreme that they name: `expert_ids`: in the 128 rows of one device no expert is named more than 28 times, a bound that some block reaches.
All inputs are finite; a program needn't handle non-finite values.
Results may differ from the reference program's by a relative error of at most 0.024.
The reference program's roundings to bfloat16 on the way count: a program that leaves them out, or rounds other values in their place, can miss the bound.
Values may be sent and summed in bfloat16 or wider, within the bound.
No kernel may reach another device: no remote copies, remote signals or barrier semaphores. Data moves between devices by JAX's collectives and lax.ppermute only.
A program may use at most 128 MiB of HBM per device.

```python
import math
import jax
import jax.numpy as jnp
import numpy as np
from jax import lax

HEADS = 20
HEAD_DIM = 128
D = 2560
HID = 832
QUERIES = 256
PATCHES = 1024
TOP = 6
EXPERTS = 32
TOK_DEV = 128
FRAMES = 128
TOKENS = 32768
CAPACITY = 28
N_DP = 8
N_EXPERT = 32


def query_table(key):
    return jax.random.truncated_normal(key, -6.0, 6.0, (QUERIES, D), jnp.float32)


def draw_queries(key, part):
    table = query_table(key)
    return table.astype(jnp.bfloat16)


def draw_patch_keys(key, part):
    key = jax.random.fold_in(key, 7)
    total_rows = FRAMES * PATCHES
    base = jax.random.truncated_normal(key, -6.0, 6.0, (total_rows, D), jnp.float32)
    return base.astype(jnp.bfloat16)


def block_levels(own_key, extent, split, low, largest):
    loudness = 1.0
    for axis_at, blocks in split:
        draws = jax.random.uniform(jax.random.fold_in(jax.random.fold_in(own_key, 6), axis_at), (blocks,), jnp.float32, low / len(split), largest / len(split))
        loudness = loudness * jnp.repeat(jnp.exp(draws), extent[axis_at] // blocks).reshape((-1,) + (1,) * (len(extent) - 1 - axis_at))
    return loudness


def shared_out(rng, own, number, rows, number_of, top, limit, lean):
    sequence = jax.random.permutation(rng, number_of)
    heavy_load, common = portions_of(number_of, rows * top, limit, lean, True), portions_of(number_of, rows * top, limit, lean, False)
    places = jnp.arange(number_of)

    def named(tallies, rotation):
        used = int((tallies > 0).sum())
        fixed = max(1, used // 4)
        shifted = fixed + (places - fixed + rotation * (used - fixed)) % max(1, number_of - fixed)
        return jnp.zeros((number_of,), jnp.int32).at[sequence[jnp.where(places < fixed, places, shifted)]].set(jnp.asarray(tallies, jnp.int32))

    tallies = jnp.where(number % 4 == 0, named(heavy_load, number // 4), named(common, number - number // 4 - 1))
    mixed = jax.random.permutation(jax.random.fold_in(own, 3), number_of)
    donor, receiver = mixed[0:number_of // 2 * 2:2], mixed[1:number_of // 2 * 2:2]
    margin = jnp.minimum(tallies[donor] - 1, limit - tallies[receiver]) // 2
    margin = jnp.where((donor == sequence[0]) | (receiver == sequence[0]) | (tallies[receiver] == 0), 0, jnp.maximum(margin, 0))
    shifted = jax.random.randint(jax.random.fold_in(own, 4), (number_of // 2,), 0, 1 << 20) % (margin + 1)
    tallies = tallies.at[donor].add(-shifted).at[receiver].add(shifted)
    members = jnp.searchsorted(jnp.cumsum(tallies), jnp.arange(rows * top), side="right").astype(jnp.int32)
    table = members.reshape(top, rows).T
    table = table[jax.random.permutation(jax.random.fold_in(own, 1), rows)]
    rotation = jax.random.randint(jax.random.fold_in(own, 2), (rows, 1), 0, top)
    return jnp.take_along_axis(table, (jnp.arange(top)[None, :] + rotation) % top, axis=1)


def portions_of(amount, total, limit, lean, full):
    portions = [(1 << 20) // math.isqrt(standing ** lean) + 1 for standing in range(1, amount + 1)]
    largest = limit if full else min(limit, max(-(-total // amount), total * portions[0] // sum(portions)))
    least = 1 if total - largest >= amount - 1 else 0
    holding, surplus = [largest] + [least] * (amount - 1), total - largest - least * (amount - 1)
    while surplus > 0:
        candidates = [i for i in range(1, amount) if holding[i] < largest] or [i for i in range(1, amount) if holding[i] < limit]
        whole, budget = sum([portions[i] for i in candidates]), surplus
        for i in candidates:
            addition = min(limit - holding[i], max(1, budget * portions[i] // whole), surplus)
            holding[i] = holding[i] + addition
            surplus = surplus - addition
    return np.array(holding)


def centred(rng, dims, scale, most, split=(), kind=jnp.bfloat16):
    array = jax.random.normal(rng, dims, jnp.float32) * scale
    if len(split) > 0:
        array = block_levels(rng, dims, split, -0.22, 0.18) * array
    return jnp.clip(array, min=-most, max=most).astype(kind)


def setup_inputs(seed: int = 0) -> dict:
    arg_keys = jax.random.split(jax.random.key(seed), 11)
    queries = draw_queries(jax.random.fold_in(arg_keys[10], 71), 0)
    patch_keys = draw_patch_keys(jax.random.fold_in(arg_keys[10], 71), 0)
    patch_values = centred(arg_keys[2], (FRAMES * PATCHES, D), 1.0, 6.0, ((0, 256),))
    norm_gain = jnp.clip(1.0 + 0.15 * jax.random.normal(arg_keys[3], (D,), jnp.float32), 0.25, 1.75)
    gate_weight = centred(arg_keys[4], (EXPERTS, D, HID), D ** -0.5, 0.125, ((0, 32), (1, 8)))
    up_weight = centred(arg_keys[5], (EXPERTS, D, HID), D ** -0.5, 0.125, ((0, 32), (1, 8)))
    down_weight = centred(arg_keys[6], (EXPERTS, HID, D), HID ** -0.5, 0.21875, ((0, 32), (2, 8)))
    expert_ids_keys = jax.random.split(jax.random.fold_in(arg_keys[7], 1), TOKENS // TOK_DEV)
    expert_ids_turns = jax.random.permutation(jax.random.fold_in(arg_keys[7], 3), TOKENS // TOK_DEV)
    expert_ids = jax.vmap(lambda own, number: shared_out(jax.random.fold_in(arg_keys[7], 2), own, number, TOK_DEV, EXPERTS, TOP, CAPACITY, 1))(expert_ids_keys, expert_ids_turns).reshape((TOKENS, TOP))
    combine_weights = jnp.clip(0.1 + 0.9 * jax.random.uniform(arg_keys[8], (TOKENS, TOP), jnp.float32) ** block_levels(arg_keys[8], (TOKENS, TOP), ((0, 256),), -0.2, 0.2), 0.1, 1.0)
    latent_grad = centred(arg_keys[9], (TOKENS, D), 1.0, 6.0, ((0, 256),))
    return dict(queries=queries, patch_keys=patch_keys, patch_values=patch_values, norm_gain=norm_gain, gate_weight=gate_weight, up_weight=up_weight, down_weight=down_weight, expert_ids=expert_ids, combine_weights=combine_weights, latent_grad=latent_grad)


EPSILON = 1e-06

def rms_scale(values, gain):
    wide = values.astype(jnp.float32)
    factor = lax.rsqrt(lax.optimization_barrier(jnp.mean(wide * wide, axis=-1, keepdims=True)) + EPSILON)
    return (wide * factor * gain).astype(jnp.bfloat16)

def reference(queries, patch_keys, patch_values, norm_gain, gate_weight, up_weight, down_weight, expert_ids, combine_weights, latent_grad):
    score_scale = 1.0 / HEAD_DIM ** 0.5
    head_queries = queries.astype(jnp.float32).reshape(QUERIES, HEADS, HEAD_DIM)
    frame_keys = patch_keys.reshape(FRAMES, PATCHES, HEADS, HEAD_DIM)
    frame_values = patch_values.reshape(FRAMES, PATCHES, HEADS, HEAD_DIM)
    frame_grads = latent_grad.reshape(FRAMES, QUERIES, HEADS, HEAD_DIM)

    def frame_step(carried, frame_item):
        keys_frame, values_frame, grads_frame = frame_item
        keys_wide = keys_frame.astype(jnp.float32)
        values_wide = values_frame.astype(jnp.float32)
        grads_wide = grads_frame.astype(jnp.float32)
        scores = jnp.einsum('qhd,khd->hqk', head_queries, keys_wide) * score_scale
        peak = lax.optimization_barrier(jnp.max(scores, axis=2, keepdims=True))
        exponent = jnp.exp(scores - peak)
        softmax_weights = exponent / lax.optimization_barrier(jnp.sum(exponent, axis=2, keepdims=True))
        rounded = lax.optimization_barrier(softmax_weights.astype(jnp.bfloat16)).astype(jnp.float32)
        attended = jnp.einsum('hqk,khd->qhd', rounded, values_wide)
        latent_rows = attended.astype(jnp.bfloat16)
        value_dot = jnp.einsum('qhd,khd->hqk', grads_wide, values_wide)
        inner_dot = jnp.einsum('qhd,qhd->hq', grads_wide, latent_rows.astype(jnp.float32))
        score_grad = (softmax_weights * (value_dot - inner_dot[:, :, None]) * score_scale).astype(jnp.bfloat16)
        score_wide = lax.optimization_barrier(score_grad).astype(jnp.float32)
        query_part = jnp.einsum('hqk,khd->qhd', score_wide, keys_wide)
        return (carried + query_part, latent_rows)
    start = jnp.zeros((QUERIES, HEADS, HEAD_DIM), jnp.float32)
    query_sum, latent_frames = lax.scan(frame_step, start, (frame_keys, frame_values, frame_grads))
    latents = latent_frames.reshape(TOKENS, D)
    normed = rms_scale(latents, norm_gain)
    devices = N_DP * N_EXPERT
    block_ids = expert_ids.reshape(devices, TOK_DEV * TOP)
    onehot = (block_ids[:, :, None] == jnp.arange(EXPERTS, dtype=jnp.int32)[None, None, :]).astype(jnp.int32)
    slot_index = lax.optimization_barrier(jnp.sum((jnp.cumsum(onehot, axis=1, dtype=jnp.int32) - 1) * onehot, axis=2, dtype=jnp.int32))
    token_index = (jnp.arange(TOKENS * TOP, dtype=jnp.int32) // TOP).reshape(devices, TOK_DEV * TOP)
    device_index = jnp.broadcast_to(jnp.arange(devices, dtype=jnp.int32)[:, None], block_ids.shape)
    table = jnp.full((devices, EXPERTS, CAPACITY), -1, jnp.int32).at[device_index, block_ids, slot_index].set(token_index)
    weight_table = jnp.zeros((devices, EXPERTS, CAPACITY), jnp.float32).at[device_index, block_ids, slot_index].set(combine_weights.reshape(devices, TOK_DEV * TOP))

    def expert_step(accumulated, expert_item):
        gate_matrix, up_matrix, down_matrix, table_expert, weight_expert = expert_item
        flat_index = table_expert.reshape(-1)
        live = flat_index >= 0
        safe_index = jnp.maximum(flat_index, 0)
        rows_in = jnp.where(live[:, None], normed[safe_index], jnp.zeros((), normed.dtype))
        gate_act = jnp.dot(rows_in, gate_matrix, preferred_element_type=jnp.float32)
        up_act = jnp.dot(rows_in, up_matrix, preferred_element_type=jnp.float32)
        hidden = (jax.nn.silu(gate_act) * up_act).astype(jnp.bfloat16)
        result = jnp.dot(hidden, down_matrix, preferred_element_type=jnp.float32).astype(jnp.bfloat16)
        entry_weights = jnp.where(live, weight_expert.reshape(-1), jnp.zeros((), weight_expert.dtype))
        accumulated = accumulated.at[safe_index].add(entry_weights[:, None] * result.astype(jnp.float32))
        return (accumulated, None)
    moe_start = jnp.zeros((TOKENS, D), jnp.float32)
    moe_sum, unused = lax.scan(expert_step, moe_start, (gate_weight, up_weight, down_weight, jnp.transpose(table, (1, 0, 2)), jnp.transpose(weight_table, (1, 0, 2))))
    layer_out = (latents.astype(jnp.float32) + moe_sum).astype(jnp.bfloat16)
    return (layer_out, query_sum.reshape(QUERIES, D))
```

```python
import functools
import math

import jax
import jax.numpy as jnp
from jax import lax
from jax.experimental import pallas as pl
from jax.experimental.pallas import tpu as pltpu
from jax.sharding import PartitionSpec as P

HEADS = 20
HEAD_DIM = 128
WIDTH = HEADS * HEAD_DIM
ROWS = 128
PATCHES = 512
TOP = 6
EXPERTS = 32
HID = 832
CAPACITY = 28
N_DP = 8
SHARD = WIDTH // N_DP
PARTS = 4
PART = WIDTH // PARTS
BLOCK = PARTS * CAPACITY
GROUP = 4
GROUP_ROWS = GROUP * BLOCK
GROUP_SLOTS = GROUP * CAPACITY
GROUPS = EXPERTS // GROUP
SLOTS = EXPERTS * CAPACITY
EPSILON = 1e-06
SCALE = 1.0 / math.sqrt(HEAD_DIM)
HEADS_PER_STEP = 2
VMEM_LIMIT = 56 * 1024 * 1024

F32 = jnp.float32
BF16 = jnp.bfloat16


def dot(a, b):
    return jnp.dot(a, b, preferred_element_type=F32)


def dot_t(a, b):
    return lax.dot_general(a, b, (((1,), (1,)), ((), ())), preferred_element_type=F32)


def iota(shape, axis):
    return lax.broadcasted_iota(jnp.int32, shape, axis)


def over_28(value):
    return (value * 1171) >> 15


def over_112(value):
    return (value * 1171) >> 17


def head_weights(queries, near_keys, far_keys):
    near = dot_t(queries, near_keys) * SCALE
    far = dot_t(queries, far_keys) * SCALE
    peak = jnp.maximum(
        jnp.max(near, axis=1, keepdims=True), jnp.max(far, axis=1, keepdims=True)
    )
    near = jnp.exp(near - peak)
    far = jnp.exp(far - peak)
    total = jnp.sum(near, axis=1, keepdims=True) + jnp.sum(far, axis=1, keepdims=True)
    inverse = 1.0 / total
    return near * inverse, far * inverse


def forward_kernel(parity, queries, near_keys, far_keys, near_values, far_values, latents):
    for head in range(HEADS_PER_STEP):
        at = slice(head * HEAD_DIM, (head + 1) * HEAD_DIM)
        near, far = head_weights(queries[:, at], near_keys[:, at], far_keys[:, at])
        attended = dot(near.astype(BF16), near_values[:, at]) + dot(
            far.astype(BF16), far_values[:, at]
        )
        latents[:, at] = attended.astype(BF16)


def backward_kernel(
    parity, queries, near_keys, far_keys, near_values, far_values, latents, cotangent, grad
):
    for head in range(HEADS_PER_STEP):
        at = slice(head * HEAD_DIM, (head + 1) * HEAD_DIM)
        near, far = head_weights(queries[:, at], near_keys[:, at], far_keys[:, at])
        given = cotangent[:, at]
        inner = jnp.sum(
            given.astype(F32) * latents[:, at].astype(F32), axis=1, keepdims=True
        )
        near = near * (dot_t(given, near_values[:, at]) - inner) * SCALE
        far = far * (dot_t(given, far_values[:, at]) - inner) * SCALE
        grad[:, at] = dot(near.astype(BF16), near_keys[:, at]) + dot(
            far.astype(BF16), far_keys[:, at]
        )


def attention(kernel, out_type, flops, parity, queries, keys, far_keys, values, far_values, *more):
    wide = HEADS_PER_STEP * HEAD_DIM
    own = pl.BlockSpec((ROWS, wide), lambda i, parity: (0, i))
    patches = pl.BlockSpec((PATCHES, wide), lambda i, parity: (0, i))
    asked = pl.BlockSpec((ROWS, wide), lambda i, parity: (parity[0], i))
    return pl.pallas_call(
        kernel,
        out_shape=jax.ShapeDtypeStruct((ROWS, WIDTH), out_type),
        grid_spec=pltpu.PrefetchScalarGridSpec(
            num_scalar_prefetch=1,
            grid=(HEADS // HEADS_PER_STEP,),
            in_specs=[asked, patches, patches, patches, patches] + [own] * len(more),
            out_specs=own,
        ),
        compiler_params=pltpu.CompilerParams(vmem_limit_bytes=VMEM_LIMIT),
        cost_estimate=pl.CostEstimate(
            flops=flops, bytes_accessed=13_000_000, transcendentals=2_621_440
        ),
    )(parity, queries, keys, far_keys, values, far_values, *more)


def slot_table(ids):
    named = jnp.zeros((ROWS, EXPERTS), F32)
    for choice in range(TOP):
        named = named + (ids[:, choice : choice + 1] == iota((ROWS, EXPERTS), 1)).astype(F32)
    earlier = (iota((ROWS, ROWS), 0) > iota((ROWS, ROWS), 1)).astype(BF16)
    before = dot(earlier, named.astype(BF16))
    return jnp.where(named > 0, before, -1.0)


def dispatch_kernel(latents, gain, ids, out, stacked):
    wide = latents[...].astype(F32)
    factor = lax.rsqrt(jnp.mean(wide * wide, axis=1, keepdims=True) + EPSILON)
    normed = (wide * factor * gain[...]).astype(BF16)
    for part in range(PARTS):
        stacked[part * ROWS : (part + 1) * ROWS, :] = normed[:, part * PART : (part + 1) * PART]
    slots = slot_table(ids).astype(BF16)
    row = iota((GROUP_ROWS, 1), 0)
    expert_of = over_112(row)
    slot_of = row - over_28(row) * CAPACITY
    part_of = over_28(row) - expert_of * PARTS
    lane_part = iota((GROUP_ROWS, PARTS * ROWS), 1) >> 7
    right_part = lane_part == part_of

    def group(g, carry):
        pick = (iota((GROUP_ROWS, EXPERTS), 1) == expert_of + g * GROUP).astype(BF16)
        place = dot_t(pick, slots)
        match = jnp.concatenate([place] * PARTS, axis=1) == slot_of.astype(F32)
        chosen = jnp.where(match & right_part, 1.0, 0.0).astype(BF16)
        at = pl.multiple_of(g * GROUP_ROWS, GROUP_ROWS)
        out[pl.ds(at, GROUP_ROWS), :] = dot(chosen, stacked[...]).astype(BF16)
        return carry

    lax.fori_loop(0, GROUPS, group, 0)


def dispatch(latents, gain, ids):
    return pl.pallas_call(
        dispatch_kernel,
        out_shape=jax.ShapeDtypeStruct((EXPERTS * BLOCK, PART), BF16),
        scratch_shapes=[pltpu.VMEM((PARTS * ROWS, PART), BF16)],
        compiler_params=pltpu.CompilerParams(vmem_limit_bytes=VMEM_LIMIT),
        cost_estimate=pl.CostEstimate(
            flops=2_400_000_000, bytes_accessed=6_000_000, transcendentals=0
        ),
    )(latents, gain, ids)


def spread_rows():
    row = iota((GROUP_ROWS, GROUP_ROWS), 0)
    part = over_112(row)
    block = over_28(row) - part * GROUP
    slot = row - over_28(row) * CAPACITY
    target = block * BLOCK + part * CAPACITY + slot
    return (iota((GROUP_ROWS, GROUP_ROWS), 1) == target).astype(BF16)


def gathered_rows():
    row = iota((GROUP_ROWS, GROUP_ROWS), 0)
    block = over_112(row)
    part = over_28(row) - block * PARTS
    slot = row - over_28(row) * CAPACITY
    target = part * GROUP_SLOTS + block * CAPACITY + slot
    return (iota((GROUP_ROWS, GROUP_ROWS), 1) == target).astype(BF16)


def open_blocks(blocks, rows):
    order = spread_rows()

    def group(g, carry):
        at = pl.multiple_of(g * GROUP_ROWS, GROUP_ROWS)
        found = dot(order, blocks[pl.ds(at, GROUP_ROWS), :]).astype(BF16)
        to = pl.multiple_of(g * GROUP_SLOTS, GROUP_SLOTS)
        for part in range(PARTS):
            rows[pl.ds(to, GROUP_SLOTS), part * PART : (part + 1) * PART] = found[
                part * GROUP_SLOTS : (part + 1) * GROUP_SLOTS, :
            ]
        return carry

    lax.fori_loop(0, GROUPS, group, 0)


HALF = SLOTS // 2


def hidden_kernel(
    place, received, own, f1, f2, f3, b1, b2, b3, gate4, up4, hidden, gate_full, up_full, rows, sems
):
    copies = []

    def bring(source, target, shard):
        at = pl.multiple_of(lax.rem(shard + N_DP, N_DP) * SHARD, SHARD)
        copy = pltpu.make_async_copy(
            source, target.at[pl.ds(at, SHARD), :], sems.at[len(copies)]
        )
        copy.start()
        copies.append(copy)

    z = place[0]
    for source, shard in (
        (own, z), (f1, z - 1), (b1, z + 1), (f2, z - 2), (b2, z + 2), (f3, z - 3), (b3, z + 3),
    ):
        bring(source.at[pl.ds(0, SHARD), :], gate_full, shard)
        bring(source.at[pl.ds(SHARD, SHARD), :], up_full, shard)
    bring(gate4, gate_full, z + 4)
    bring(up4, up_full, z + 4)
    open_blocks(received, rows)
    for copy in copies:
        copy.wait()

    def half(h, carry):
        at = pl.multiple_of(h * HALF, HALF)
        taken = rows[pl.ds(at, HALF), :]
        gate = dot(taken, gate_full[...])
        up = dot(taken, up_full[...])
        hidden[pl.ds(at, HALF), :] = (gate / (1.0 + jnp.exp(-gate)) * up).astype(BF16)
        return carry

    lax.fori_loop(0, 2, half, 0)


def hidden_units(place, received, own, forth, back, gate4, up4):
    smem = pl.BlockSpec(memory_space=pltpu.SMEM)
    vmem = pl.BlockSpec(memory_space=pltpu.VMEM)
    hbm = pl.BlockSpec(memory_space=pl.ANY)
    return pl.pallas_call(
        hidden_kernel,
        out_shape=jax.ShapeDtypeStruct((SLOTS, HID), BF16),
        in_specs=[smem, vmem] + [hbm] * 9,
        out_specs=vmem,
        scratch_shapes=[
            pltpu.VMEM((WIDTH, HID), BF16),
            pltpu.VMEM((WIDTH, HID), BF16),
            pltpu.VMEM((SLOTS, WIDTH), BF16),
            pltpu.SemaphoreType.DMA((16,)),
        ],
        compiler_params=pltpu.CompilerParams(vmem_limit_bytes=VMEM_LIMIT),
        cost_estimate=pl.CostEstimate(
            flops=9_700_000_000, bytes_accessed=15_000_000, transcendentals=745_472
        ),
    )(place, received, own, *forth, *back, gate4, up4)


def result_kernel(place, hidden, own, f1, f2, f3, b1, b2, b3, low4, high4, out, full, rows, sems):
    copies = []

    def bring(source, shard, offset, count):
        at = pl.multiple_of(lax.rem(shard + N_DP, N_DP) * SHARD + offset, 32)
        copy = pltpu.make_async_copy(source, full.at[pl.ds(at, count), :], sems.at[len(copies)])
        copy.start()
        copies.append(copy)

    z = place[0]
    for source, shard in (
        (own, z), (f1, z - 1), (b1, z + 1), (f2, z - 2), (b2, z + 2), (f3, z - 3), (b3, z + 3),
    ):
        bring(source, shard, 0, SHARD)
    bring(low4, z + 4, 0, SHARD // 2)
    bring(high4, z + 4, SHARD // 2, SHARD // 2)
    for copy in copies:
        copy.wait()

    def half(h, carry):
        at = pl.multiple_of(h * HALF, HALF)
        rows[pl.ds(at, HALF), :] = dot_t(hidden[pl.ds(at, HALF), :], full[...]).astype(BF16)
        return carry

    lax.fori_loop(0, 2, half, 0)
    order = gathered_rows()

    def group(g, carry):
        at = pl.multiple_of(g * GROUP_SLOTS, GROUP_SLOTS)
        taken = jnp.concatenate(
            [
                rows[pl.ds(at, GROUP_SLOTS), part * PART : (part + 1) * PART]
                for part in range(PARTS)
            ],
            axis=0,
        )
        to = pl.multiple_of(g * GROUP_ROWS, GROUP_ROWS)
        out[pl.ds(to, GROUP_ROWS), :] = dot(order, taken).astype(BF16)
        return carry

    lax.fori_loop(0, GROUPS, group, 0)


def results(place, hidden, own, forth, back, low4, high4):
    smem = pl.BlockSpec(memory_space=pltpu.SMEM)
    vmem = pl.BlockSpec(memory_space=pltpu.VMEM)
    hbm = pl.BlockSpec(memory_space=pl.ANY)
    return pl.pallas_call(
        result_kernel,
        out_shape=jax.ShapeDtypeStruct((EXPERTS * BLOCK, PART), BF16),
        in_specs=[smem, vmem] + [hbm] * 9,
        out_specs=vmem,
        scratch_shapes=[
            pltpu.VMEM((WIDTH, HID), BF16),
            pltpu.VMEM((SLOTS, WIDTH), BF16),
            pltpu.SemaphoreType.DMA((9,)),
        ],
        compiler_params=pltpu.CompilerParams(vmem_limit_bytes=VMEM_LIMIT),
        cost_estimate=pl.CostEstimate(
            flops=5_900_000_000, bytes_accessed=11_000_000, transcendentals=0
        ),
    )(place, hidden, own, *forth, *back, low4, high4)


def combine_kernel(returned, latents, ids, weights, out, rows):
    open_blocks(returned, rows)
    slots = slot_table(ids)
    shares = jnp.zeros((ROWS, EXPERTS), F32)
    for choice in range(TOP):
        named = ids[:, choice : choice + 1] == iota((ROWS, EXPERTS), 1)
        shares = shares + jnp.where(named, weights[:, choice : choice + 1], 0.0)
    high = shares.astype(BF16)
    rest = shares - high.astype(F32)
    middle = rest.astype(BF16)
    low = (rest - middle.astype(F32)).astype(BF16)
    row = iota((EXPERTS, SLOTS), 1)
    pick = (over_28(row) == iota((EXPERTS, SLOTS), 0)).astype(BF16)
    lane = iota((ROWS, SLOTS), 1)
    slot_of = (lane - over_28(lane) * CAPACITY).astype(F32)
    match = dot(slots.astype(BF16), pick) == slot_of
    terms = [
        jnp.where(match, dot(term, pick), 0.0).astype(BF16) for term in (high, middle, low)
    ]
    stacked = jnp.concatenate(terms, axis=0)
    for part in range(PARTS):
        at = slice(part * PART, (part + 1) * PART)
        found = dot(stacked, rows[:, at])
        mixed = found[:ROWS] + (found[ROWS : 2 * ROWS] + found[2 * ROWS :])
        out[:, at] = (latents[:, at].astype(F32) + mixed).astype(BF16)


def combine(returned, latents, ids, weights):
    return pl.pallas_call(
        combine_kernel,
        out_shape=jax.ShapeDtypeStruct((ROWS, WIDTH), BF16),
        scratch_shapes=[pltpu.VMEM((SLOTS, WIDTH), BF16)],
        compiler_params=pltpu.CompilerParams(vmem_limit_bytes=VMEM_LIMIT),
        cost_estimate=pl.CostEstimate(
            flops=4_000_000_000, bytes_accessed=6_000_000, transcendentals=0
        ),
    )(returned, latents, ids, weights)


SAME_CORE = [list(range(core, EXPERTS, 2)) for core in range(2)]


def other_core(value):
    return lax.ppermute(value, "expert", [(at, at ^ 1) for at in range(EXPERTS)])


def along(value, step):
    return lax.ppermute(value, "dp", [(at, (at + step) % N_DP) for at in range(N_DP)])


def ring(own):
    forth, back = [], []
    ahead = behind = own
    for _ in range(3):
        ahead, behind = along(ahead, 1), along(behind, -1)
        forth.append(ahead)
        back.append(behind)
    middle = own.shape[0] // 2
    return forth, back, along(ahead[:middle], 1), along(behind[middle:], -1)


def summed(part):
    pieces = lax.all_to_all(
        part.reshape(EXPERTS // 2, -1, WIDTH),
        "expert",
        split_axis=0,
        concat_axis=0,
        tiled=True,
        axis_index_groups=SAME_CORE,
    )
    total = jnp.sum(pieces, axis=0)
    for bit in (1, 2, 4):
        total = total + lax.ppermute(total, "dp", [(at, at ^ bit) for at in range(N_DP)])
    half = lax.all_gather(total, "expert", axis=0, tiled=True, axis_index_groups=SAME_CORE)
    return half, other_core(half)


def per_device(
    queries,
    patch_keys,
    patch_values,
    norm_gain,
    gate_weight,
    up_weight,
    down_weight,
    expert_ids,
    combine_weights,
    latent_grad,
):
    parity = lax.axis_index("expert") % 2
    which = parity.reshape(1).astype(jnp.int32)
    place = lax.axis_index("dp").reshape(1).astype(jnp.int32)
    far_keys, far_values = other_core(patch_keys), other_core(patch_values)
    gate_up = jnp.concatenate([gate_weight[0], up_weight[0]], axis=0)
    down = down_weight[0].T
    both = ring(gate_up)
    downs = ring(down)
    patches = (which, queries, patch_keys, far_keys, patch_values, far_values)
    latents = attention(forward_kernel, BF16, 1_342_177_280, *patches)
    sent = dispatch(latents, norm_gain.reshape(1, WIDTH), expert_ids)
    received = lax.all_to_all(
        sent.reshape(EXPERTS, BLOCK, PART), "expert", split_axis=0, concat_axis=0, tiled=True
    ).reshape(EXPERTS * BLOCK, PART)
    grad_part = attention(
        backward_kernel, F32, 2_684_354_560, *patches, latents, latent_grad
    )
    hidden = hidden_units(place, received, gate_up, *both)
    result = results(place, hidden, down, *downs)
    returned = lax.all_to_all(
        result.reshape(EXPERTS, BLOCK, PART), "expert", split_axis=0, concat_axis=0, tiled=True
    ).reshape(EXPERTS * BLOCK, PART)
    half, far_half = summed(grad_part)
    first = jnp.where(parity == 0, half, far_half)
    second = jnp.where(parity == 0, far_half, half)
    query_grad = jnp.concatenate([first, second], axis=0)
    layer_out = combine(returned, latents, expert_ids, combine_weights)
    return (layer_out, query_grad)


def solution(mesh):
    return jax.shard_map(
        per_device,
        mesh=mesh,
        in_specs=(
            P(),
            P(("dp", "expert"), None),
            P(("dp", "expert"), None),
            P(),
            P("expert", "dp", None),
            P("expert", "dp", None),
            P("expert", None, "dp"),
            P(("dp", "expert"), None),
            P(("dp", "expert"), None),
            P(("dp", "expert"), None),
        ),
        out_specs=(P(("dp", "expert"), None), P()),
        check_vma=False,
    )
```

```python
import functools
import math

import jax
import jax.numpy as jnp
from jax import lax
from jax.experimental import pallas as pl
from jax.experimental.pallas import tpu as pltpu
from jax.sharding import PartitionSpec as P

HEADS = 20
HEAD_DIM = 128
WIDTH = HEADS * HEAD_DIM
ROWS = 128
PATCHES = 512
TOP = 6
EXPERTS = 32
HID = 832
CAPACITY = 28
N_DP = 8
SHARD = WIDTH // N_DP
HALVES = 2
BLOCK = HALVES * CAPACITY
GROUP = 8
GROUPS = EXPERTS // GROUP
GROUP_ROWS = GROUP * BLOCK
SMALL = 4
SMALL_ROWS = SMALL * BLOCK
SMALL_SLOTS = SMALL * CAPACITY
SLOTS = EXPERTS * CAPACITY
CHUNK = WIDTH // 2
SPLIT = (128, SHARD - 128)
EPSILON = 1e-06
SCALE = 1.0 / math.sqrt(HEAD_DIM)
HEADS_PER_STEP = 4
VMEM_LIMIT = 56 * 1024 * 1024

F32 = jnp.float32
BF16 = jnp.bfloat16


def dot(a, b):
    return jnp.dot(a, b, preferred_element_type=F32)


def dot_t(a, b):
    return lax.dot_general(a, b, (((1,), (1,)), ((), ())), preferred_element_type=F32)


def iota(shape, axis):
    return lax.broadcasted_iota(jnp.int32, shape, axis)


def over_28(value):
    return (value * 1171) >> 15


def over_56(value):
    return (value * 1171) >> 16


def head_weights(queries, near_keys, far_keys):
    near = dot_t(queries, near_keys) * SCALE
    far = dot_t(queries, far_keys) * SCALE
    peak = jnp.maximum(
        jnp.max(near, axis=1, keepdims=True), jnp.max(far, axis=1, keepdims=True)
    )
    near = jnp.exp(near - peak)
    far = jnp.exp(far - peak)
    total = jnp.sum(near, axis=1, keepdims=True) + jnp.sum(far, axis=1, keepdims=True)
    inverse = 1.0 / total
    return near * inverse, far * inverse


def attention_kernel(
    parity, queries, near_keys, far_keys, near_values, far_values, cotangent, latents, grad
):
    for head in range(HEADS_PER_STEP):
        at = slice(head * HEAD_DIM, (head + 1) * HEAD_DIM)
        near, far = head_weights(queries[:, at], near_keys[:, at], far_keys[:, at])
        attended = dot(near.astype(BF16), near_values[:, at]) + dot(
            far.astype(BF16), far_values[:, at]
        )
        rounded = attended.astype(BF16)
        latents[:, at] = rounded
        given = cotangent[:, at]
        inner = jnp.sum(given.astype(F32) * rounded.astype(F32), axis=1, keepdims=True)
        near = near * (dot_t(given, near_values[:, at]) - inner) * SCALE
        far = far * (dot_t(given, far_values[:, at]) - inner) * SCALE
        part = dot(near.astype(BF16), near_keys[:, at]) + dot(far.astype(BF16), far_keys[:, at])
        grad[:, at] = part.astype(BF16)


def attention(parity, queries, keys, far_keys, values, far_values, cotangent):
    wide = HEADS_PER_STEP * HEAD_DIM
    own = pl.BlockSpec((ROWS, wide), lambda i, parity: (0, i))
    patches = pl.BlockSpec((PATCHES, wide), lambda i, parity: (0, i))
    asked = pl.BlockSpec((ROWS, wide), lambda i, parity: (parity[0], i))
    return pl.pallas_call(
        attention_kernel,
        out_shape=(
            jax.ShapeDtypeStruct((ROWS, WIDTH), BF16),
            jax.ShapeDtypeStruct((ROWS, WIDTH), BF16),
        ),
        grid_spec=pltpu.PrefetchScalarGridSpec(
            num_scalar_prefetch=1,
            grid=(HEADS // HEADS_PER_STEP,),
            in_specs=[asked, patches, patches, patches, patches, own],
            out_specs=(own, own),
        ),
        compiler_params=pltpu.CompilerParams(vmem_limit_bytes=VMEM_LIMIT),
        cost_estimate=pl.CostEstimate(
            flops=2_684_354_560, bytes_accessed=13_000_000, transcendentals=2_621_440
        ),
    )(parity, queries, keys, far_keys, values, far_values, cotangent)


def slot_table(ids):
    named = jnp.zeros((ROWS, EXPERTS), F32)
    for choice in range(TOP):
        named = named + (ids[:, choice : choice + 1] == iota((ROWS, EXPERTS), 1)).astype(F32)
    earlier = (iota((ROWS, ROWS), 0) > iota((ROWS, ROWS), 1)).astype(BF16)
    before = dot(earlier, named.astype(BF16))
    return jnp.where(named > 0, before, -1.0)


def dispatch_kernel(latents, gain, ids, out, stacked, slots):
    at_group = pl.program_id(0)

    @pl.when(at_group == 0)
    def _():
        wide = latents[...].astype(F32)
        factor = lax.rsqrt(jnp.mean(wide * wide, axis=1, keepdims=True) + EPSILON)
        normed = (wide * factor * gain[...]).astype(BF16)
        stacked[:ROWS, :] = normed[:, :CHUNK]
        stacked[ROWS:, :] = normed[:, CHUNK:]
        slots[...] = slot_table(ids).astype(BF16)

    row = iota((GROUP_ROWS, 1), 0)
    expert_of = over_56(row)
    slot_of = row - over_28(row) * CAPACITY
    half_of = over_28(row) - expert_of * HALVES
    pick = (iota((GROUP_ROWS, EXPERTS), 1) == expert_of + at_group * GROUP).astype(BF16)
    match = dot_t(pick, slots[...]) == slot_of.astype(F32)
    chosen = jnp.concatenate(
        [jnp.where(match & (half_of == half), 1.0, 0.0) for half in range(HALVES)], axis=1
    )
    out[...] = dot(chosen.astype(BF16), stacked[...]).astype(BF16)


def dispatch(latents, gain, ids):
    return pl.pallas_call(
        dispatch_kernel,
        grid=(GROUPS,),
        in_specs=[
            pl.BlockSpec((ROWS, WIDTH), lambda i: (0, 0)),
            pl.BlockSpec((1, WIDTH), lambda i: (0, 0)),
            pl.BlockSpec((ROWS, TOP), lambda i: (0, 0)),
        ],
        out_specs=pl.BlockSpec((GROUP_ROWS, CHUNK), lambda i: (i, 0)),
        out_shape=jax.ShapeDtypeStruct((EXPERTS * BLOCK, CHUNK), BF16),
        scratch_shapes=[
            pltpu.VMEM((HALVES * ROWS, CHUNK), BF16),
            pltpu.VMEM((ROWS, EXPERTS), BF16),
        ],
        compiler_params=pltpu.CompilerParams(vmem_limit_bytes=VMEM_LIMIT),
        cost_estimate=pl.CostEstimate(
            flops=1_200_000_000, bytes_accessed=6_000_000, transcendentals=0
        ),
    )(latents, gain, ids)


def spread_rows():
    row = iota((SMALL_ROWS, SMALL_ROWS), 0)
    half = (row >= SMALL_SLOTS).astype(jnp.int32)
    slots = row - half * SMALL_SLOTS
    target = row - half * SMALL_SLOTS + over_28(slots) * CAPACITY + half * CAPACITY
    return (iota((SMALL_ROWS, SMALL_ROWS), 1) == target).astype(BF16)


def gathered_rows():
    row = iota((SMALL_ROWS, SMALL_ROWS), 0)
    block = over_56(row)
    half = over_28(row) - block * HALVES
    slot = row - over_28(row) * CAPACITY
    target = half * SMALL_SLOTS + block * CAPACITY + slot
    return (iota((SMALL_ROWS, SMALL_ROWS), 1) == target).astype(BF16)


HALF = SLOTS // 2
GATHER_ROWS = 2 * SHARD + SPLIT[0]


def whole_block(shape):
    return pl.BlockSpec(shape, lambda i: (0, 0))


def open_kernel(blocks, rows):
    order = spread_rows()
    for part in range(GROUP // SMALL):
        at, to = part * SMALL_ROWS, part * SMALL_SLOTS
        found = dot(order, blocks[at : at + SMALL_ROWS, :]).astype(BF16)
        rows[to : to + SMALL_SLOTS, :CHUNK] = found[:SMALL_SLOTS, :]
        rows[to : to + SMALL_SLOTS, CHUNK:] = found[SMALL_SLOTS:, :]


def opened(received):
    return pl.pallas_call(
        open_kernel,
        grid=(GROUPS,),
        in_specs=[pl.BlockSpec((GROUP_ROWS, CHUNK), lambda i: (i, 0))],
        out_specs=pl.BlockSpec((GROUP_ROWS // HALVES, WIDTH), lambda i: (i, 0)),
        out_shape=jax.ShapeDtypeStruct((SLOTS, WIDTH), BF16),
        compiler_params=pltpu.CompilerParams(vmem_limit_bytes=VMEM_LIMIT),
        cost_estimate=pl.CostEstimate(
            flops=1_000_000_000, bytes_accessed=9_000_000, transcendentals=0
        ),
    )(received)


def close_rows(order, rows, out):
    width = rows.shape[1] // 2
    for group in range(HALF // SMALL_SLOTS):
        taken = rows[group * SMALL_SLOTS : (group + 1) * SMALL_SLOTS, :]
        taken = jnp.concatenate([taken[:, :width], taken[:, width:]], axis=0)
        out[group * SMALL_ROWS : (group + 1) * SMALL_ROWS, :] = dot(order, taken).astype(BF16)


def expert_kernel(rows, gathered, hidden, out, taken, full, down, gates, outs, sems, out_sems):
    row_copies = [
        pltpu.make_async_copy(
            rows.at[pl.ds(half * HALF, HALF), :],
            taken.at[pl.ds(half * HALF, HALF), :],
            sems.at[half],
        )
        for half in range(2)
    ]
    gate_copies, up_copies, down_copies = [], [], []
    for shard in range(N_DP):
        for which, copies in enumerate((gate_copies, up_copies)):
            copies.append(
                pltpu.make_async_copy(
                    gathered.at[pl.ds(shard * GATHER_ROWS + which * SHARD, SHARD), :],
                    full.at[which, pl.ds(shard * SHARD, SHARD), :],
                    sems.at[2 + 3 * shard + which],
                )
            )
        down_copies.append(
            pltpu.make_async_copy(
                gathered.at[pl.ds(shard * GATHER_ROWS + 2 * SHARD, SPLIT[0]), :],
                down.at[pl.ds(shard * SPLIT[0], SPLIT[0]), :],
                sems.at[2 + 3 * shard + 2],
            )
        )
    for copy in [row_copies[0]] + gate_copies + [row_copies[1]] + up_copies + down_copies:
        copy.start()
    for copy in [row_copies[0]] + gate_copies:
        copy.wait()
    gates[:HALF, :] = dot(taken[:HALF, :], full[0])
    row_copies[1].wait()
    gates[HALF:, :] = dot(taken[HALF:, :], full[0])
    for copy in up_copies:
        copy.wait()
    for half in range(2):
        at = slice(half * HALF, (half + 1) * HALF)
        gate = gates[at, :]
        up = dot(taken[at, :], full[1])
        hidden[at, :] = (gate / (1.0 + jnp.exp(-gate)) * up).astype(BF16)
    for copy in down_copies:
        copy.wait()
    order = gathered_rows()
    out_copies = []
    for half in range(2):
        at = slice(half * HALF, (half + 1) * HALF)
        result = dot_t(hidden[at, :], down[...]).astype(BF16)
        close_rows(order, result, outs.at[half])
        copy = pltpu.make_async_copy(
            outs.at[half],
            out.at[pl.ds(half * HALF * HALVES, HALF * HALVES), :],
            out_sems.at[half],
        )
        copy.start()
        out_copies.append(copy)
    for copy in out_copies:
        copy.wait()


def experts(rows, gathered):
    columns = N_DP * SPLIT[0]
    hbm = pl.BlockSpec(memory_space=pl.ANY)
    return pl.pallas_call(
        expert_kernel,
        out_shape=(
            jax.ShapeDtypeStruct((SLOTS, HID), BF16),
            jax.ShapeDtypeStruct((EXPERTS * BLOCK, columns // 2), BF16),
        ),
        in_specs=[hbm, hbm],
        out_specs=(pl.BlockSpec(memory_space=pltpu.VMEM), hbm),
        scratch_shapes=[
            pltpu.VMEM((SLOTS, WIDTH), BF16),
            pltpu.VMEM((2, WIDTH, HID), BF16),
            pltpu.VMEM((columns, HID), BF16),
            pltpu.VMEM((SLOTS, HID), F32),
            pltpu.VMEM((2, HALF * HALVES, columns // 2), BF16),
            pltpu.SemaphoreType.DMA((2 + 3 * N_DP,)),
            pltpu.SemaphoreType.DMA((2,)),
        ],
        compiler_params=pltpu.CompilerParams(vmem_limit_bytes=VMEM_LIMIT),
        cost_estimate=pl.CostEstimate(
            flops=10_000_000_000, bytes_accessed=20_000_000, transcendentals=745_472
        ),
    )(rows, gathered)


def result_kernel(hidden, full, out):
    rows = dot_t(hidden[...], full[...]).astype(BF16)
    close_rows(gathered_rows(), rows, out)


def results(hidden, down):
    columns = down.shape[0]
    return pl.pallas_call(
        result_kernel,
        grid=(2,),
        out_shape=jax.ShapeDtypeStruct((EXPERTS * BLOCK, columns // 2), BF16),
        in_specs=[
            pl.BlockSpec((HALF, HID), lambda i: (i, 0)),
            whole_block((columns, HID)),
        ],
        out_specs=pl.BlockSpec((HALF * HALVES, columns // 2), lambda i: (i, 0)),
        compiler_params=pltpu.CompilerParams(vmem_limit_bytes=VMEM_LIMIT),
        cost_estimate=pl.CostEstimate(
            flops=3_000_000_000, bytes_accessed=8_000_000, transcendentals=0
        ),
    )(hidden, down)


TERMS = 2
SHARE_ROWS = TERMS * HALVES * ROWS


def share_kernel(ids, weights, out, slots, terms):
    at_group = pl.program_id(0)

    @pl.when(at_group == 0)
    def _():
        slots[...] = slot_table(ids).astype(BF16)
        shares = jnp.zeros((ROWS, EXPERTS), F32)
        for choice in range(TOP):
            named = ids[:, choice : choice + 1] == iota((ROWS, EXPERTS), 1)
            shares = shares + jnp.where(named, weights[:, choice : choice + 1], 0.0)
        high = shares.astype(BF16)
        terms[:ROWS, :] = high
        terms[ROWS:, :] = (shares - high.astype(F32)).astype(BF16)

    row = iota((EXPERTS, GROUP_ROWS), 1)
    pick = (over_56(row) + at_group * GROUP == iota((EXPERTS, GROUP_ROWS), 0)).astype(BF16)
    lane = iota((ROWS, GROUP_ROWS), 1)
    slot_of = lane - over_28(lane) * CAPACITY
    half_of = over_28(lane) - over_56(lane) * HALVES
    match = dot(slots[...], pick) == slot_of.astype(F32)
    shares = dot(terms[...], pick)
    for term in range(TERMS):
        for half in range(HALVES):
            at = (term * HALVES + half) * ROWS
            out[at : at + ROWS, :] = jnp.where(
                match & (half_of == half), shares[term * ROWS : (term + 1) * ROWS], 0.0
            ).astype(BF16)


def share_table(ids, weights):
    return pl.pallas_call(
        share_kernel,
        grid=(GROUPS,),
        in_specs=[whole_block((ROWS, TOP)), whole_block((ROWS, TOP))],
        out_specs=pl.BlockSpec((SHARE_ROWS, GROUP_ROWS), lambda i: (i, 0)),
        out_shape=jax.ShapeDtypeStruct((GROUPS * SHARE_ROWS, GROUP_ROWS), BF16),
        scratch_shapes=[
            pltpu.VMEM((ROWS, EXPERTS), BF16),
            pltpu.VMEM((TERMS * ROWS, EXPERTS), BF16),
        ],
        compiler_params=pltpu.CompilerParams(vmem_limit_bytes=VMEM_LIMIT),
        cost_estimate=pl.CostEstimate(
            flops=50_000_000, bytes_accessed=2_000_000, transcendentals=0
        ),
    )(ids, weights)


def mix_blocks(shares, returned, total):
    found = dot(shares[...], returned[...])
    step = HALVES * ROWS
    found = found[:step] + found[step:]

    @pl.when(pl.program_id(0) == 0)
    def _():
        total[...] = found

    @pl.when(pl.program_id(0) > 0)
    def _():
        total[...] += found


def mix_kernel(shares, returned, out, total):
    mix_blocks(shares, returned, total)

    @pl.when(pl.program_id(0) == GROUPS - 1)
    def _():
        width = returned.shape[1]
        out[:, :width] = total[:ROWS, :]
        out[:, width:] = total[ROWS:, :]


def last_kernel(shares, returned, first, latents, out, total):
    mix_blocks(shares, returned, total)

    @pl.when(pl.program_id(0) == GROUPS - 1)
    def _():
        pieces = []
        for shard in range(N_DP):
            half, at = shard // 4, shard % 4 * SPLIT[1]
            pieces.append(first[:, shard * SPLIT[0] : (shard + 1) * SPLIT[0]])
            pieces.append(total[half * ROWS : (half + 1) * ROWS, at : at + SPLIT[1]])
        whole = jnp.concatenate(pieces, axis=1)
        out[...] = (latents[...].astype(F32) + whole).astype(BF16)


def mixed(shares, returned, *last):
    width = returned.shape[1]
    specs = [
        pl.BlockSpec((SHARE_ROWS, GROUP_ROWS), lambda i: (i, 0)),
        pl.BlockSpec((GROUP_ROWS, width), lambda i: (i, 0)),
    ]
    out, kernel = jax.ShapeDtypeStruct((ROWS, 2 * width), F32), mix_kernel
    if last:
        specs += [whole_block(value.shape) for value in last]
        out, kernel = jax.ShapeDtypeStruct((ROWS, WIDTH), BF16), last_kernel
    return pl.pallas_call(
        kernel,
        grid=(GROUPS,),
        in_specs=specs,
        out_shape=out,
        out_specs=whole_block(out.shape),
        scratch_shapes=[pltpu.VMEM((HALVES * ROWS, width), F32)],
        compiler_params=pltpu.CompilerParams(vmem_limit_bytes=VMEM_LIMIT),
        cost_estimate=pl.CostEstimate(
            flops=1_200_000_000, bytes_accessed=4_000_000, transcendentals=0
        ),
    )(shares, returned, *last)


SAME_CORE = [list(range(core, EXPERTS, 2)) for core in range(2)]


def other_core(value):
    return lax.ppermute(value, "expert", [(at, at ^ 1) for at in range(EXPERTS)])


def between_chips(pieces):
    return lax.all_to_all(
        pieces,
        "expert",
        split_axis=0,
        concat_axis=0,
        tiled=True,
        axis_index_groups=SAME_CORE,
    )


def scattered(part):
    pieces = between_chips(part.reshape(EXPERTS // 2, -1, WIDTH))
    return jnp.sum(pieces.astype(F32), axis=0)


def exchange_sum(total, bit):
    return total + lax.ppermute(total, "dp", [(at, at ^ bit) for at in range(N_DP)])


def spread(total):
    pieces = jnp.broadcast_to(total.astype(BF16), (EXPERTS // 2,) + total.shape)
    return between_chips(pieces).reshape(-1, WIDTH)


def both_halves(half):
    far_half = other_core(half)
    low = lax.axis_index("expert") % 2 == 0
    whole = jnp.concatenate(
        [jnp.where(low, half, far_half), jnp.where(low, far_half, half)], axis=0
    )
    return whole.astype(F32)


def exchanged(blocks):
    rows, columns = blocks.shape
    return lax.all_to_all(
        blocks.reshape(EXPERTS, rows // EXPERTS, columns),
        "expert",
        split_axis=0,
        concat_axis=0,
        tiled=True,
    ).reshape(rows, columns)


def tied(*values):
    return lax.optimization_barrier(values)


def per_device(
    queries,
    patch_keys,
    patch_values,
    norm_gain,
    gate_weight,
    up_weight,
    down_weight,
    expert_ids,
    combine_weights,
    latent_grad,
):
    parity = lax.axis_index("expert") % 2
    which = parity.reshape(1).astype(jnp.int32)
    far_keys, far_values = other_core(patch_keys), other_core(patch_values)
    down = down_weight[0].T
    shard = jnp.concatenate([gate_weight[0], up_weight[0], down[: SPLIT[0]]], axis=0)
    gathered = lax.all_gather(shard, "dp", axis=0, tiled=True)
    patches = (which, queries, patch_keys, far_keys, patch_values, far_values)
    latents, grad_part = attention(*patches, latent_grad)
    latents, down = tied(latents, down)
    second_down = lax.all_gather(down[SPLIT[0] :], "dp", axis=0, tiled=True)
    total = scattered(grad_part)
    sent = dispatch(latents, norm_gain.reshape(1, WIDTH), expert_ids)
    sent, total, same_ids = tied(sent, total, expert_ids)
    received = exchanged(sent)
    shares = share_table(same_ids, combine_weights)
    total = exchange_sum(exchange_sum(exchange_sum(total, 1), 2), 4)
    received, total, shares = tied(received, total, shares)
    rows = opened(received)
    rows, total = tied(rows, total)
    half = spread(total)
    hidden, first = experts(rows, gathered)
    hidden, first, half = tied(hidden, first, half)
    first = exchanged(first)
    second = exchanged(results(hidden, second_down))
    first_mix = mixed(shares, first)
    layer_out = mixed(shares, second, first_mix, latents)
    query_grad = both_halves(half)
    return (layer_out, query_grad)


def solution(mesh):
    return jax.shard_map(
        per_device,
        mesh=mesh,
        in_specs=(
            P(),
            P(("dp", "expert"), None),
            P(("dp", "expert"), None),
            P(),
            P("expert", "dp", None),
            P("expert", "dp", None),
            P("expert", None, "dp"),
            P(("dp", "expert"), None),
            P(("dp", "expert"), None),
            P(("dp", "expert"), None),
        ),
        out_specs=(P(("dp", "expert"), None), P()),
        check_vma=False,
    )
```

```python
import functools
import math

import jax
import jax.numpy as jnp
from jax import lax
from jax.experimental import pallas as pl
from jax.experimental.pallas import tpu as pltpu
from jax.sharding import PartitionSpec as P

HEADS = 20
HEAD_DIM = 128
WIDTH = HEADS * HEAD_DIM
ROWS = 128
PATCHES = 512
TOP = 6
EXPERTS = 32
HID = 832
CAPACITY = 28
N_DP = 8
SHARD = WIDTH // N_DP
HALVES = 2
BLOCK = HALVES * CAPACITY
GROUP = 8
GROUPS = EXPERTS // GROUP
GROUP_ROWS = GROUP * BLOCK
SMALL = 4
SMALL_ROWS = SMALL * BLOCK
SMALL_SLOTS = SMALL * CAPACITY
SLOTS = EXPERTS * CAPACITY
CHUNK = WIDTH // 2
SPLIT = (128, SHARD - 128)
MAIN = 768
REST = HID - MAIN
FIRST_MAIN = 2 * SHARD + SPLIT[0]
FIRST_REST = 64
FIRST_ROWS = FIRST_MAIN + FIRST_REST
SECOND_REST = 16
SECOND_ROWS = SPLIT[1] + SECOND_REST
EPSILON = 1e-06
SCALE = 1.0 / math.sqrt(HEAD_DIM)
HEADS_PER_STEP = 4
VMEM_LIMIT = 56 * 1024 * 1024

F32 = jnp.float32
BF16 = jnp.bfloat16


def dot(a, b):
    return jnp.dot(a, b, preferred_element_type=F32)


def dot_t(a, b):
    return lax.dot_general(a, b, (((1,), (1,)), ((), ())), preferred_element_type=F32)


def iota(shape, axis):
    return lax.broadcasted_iota(jnp.int32, shape, axis)


def over_28(value):
    return (value * 1171) >> 15


def over_56(value):
    return (value * 1171) >> 16


def head_weights(queries, near_keys, far_keys):
    near = dot_t(queries, near_keys) * SCALE
    far = dot_t(queries, far_keys) * SCALE
    peak = jnp.maximum(
        jnp.max(near, axis=1, keepdims=True), jnp.max(far, axis=1, keepdims=True)
    )
    near = jnp.exp(near - peak)
    far = jnp.exp(far - peak)
    total = jnp.sum(near, axis=1, keepdims=True) + jnp.sum(far, axis=1, keepdims=True)
    inverse = 1.0 / total
    return near * inverse, far * inverse


def attention_kernel(
    parity, queries, near_keys, far_keys, near_values, far_values, cotangent, latents, grad
):
    for head in range(HEADS_PER_STEP):
        at = slice(head * HEAD_DIM, (head + 1) * HEAD_DIM)
        near, far = head_weights(queries[:, at], near_keys[:, at], far_keys[:, at])
        attended = dot(near.astype(BF16), near_values[:, at]) + dot(
            far.astype(BF16), far_values[:, at]
        )
        rounded = attended.astype(BF16)
        latents[:, at] = rounded
        given = cotangent[:, at]
        inner = jnp.sum(given.astype(F32) * rounded.astype(F32), axis=1, keepdims=True)
        near = near * (dot_t(given, near_values[:, at]) - inner) * SCALE
        far = far * (dot_t(given, far_values[:, at]) - inner) * SCALE
        part = dot(near.astype(BF16), near_keys[:, at]) + dot(far.astype(BF16), far_keys[:, at])
        grad[:, at] = part.astype(BF16)


def attention(parity, queries, keys, far_keys, values, far_values, cotangent):
    wide = HEADS_PER_STEP * HEAD_DIM
    own = pl.BlockSpec((ROWS, wide), lambda i, parity: (0, i))
    patches = pl.BlockSpec((PATCHES, wide), lambda i, parity: (0, i))
    asked = pl.BlockSpec((ROWS, wide), lambda i, parity: (parity[0], i))
    return pl.pallas_call(
        attention_kernel,
        out_shape=(
            jax.ShapeDtypeStruct((ROWS, WIDTH), BF16),
            jax.ShapeDtypeStruct((ROWS, WIDTH), BF16),
        ),
        grid_spec=pltpu.PrefetchScalarGridSpec(
            num_scalar_prefetch=1,
            grid=(HEADS // HEADS_PER_STEP,),
            in_specs=[asked, patches, patches, patches, patches, own],
            out_specs=(own, own),
        ),
        compiler_params=pltpu.CompilerParams(vmem_limit_bytes=VMEM_LIMIT),
        cost_estimate=pl.CostEstimate(
            flops=2_684_354_560, bytes_accessed=13_000_000, transcendentals=2_621_440
        ),
    )(parity, queries, keys, far_keys, values, far_values, cotangent)


def slot_table(ids):
    named = jnp.zeros((ROWS, EXPERTS), F32)
    for choice in range(TOP):
        named = named + (ids[:, choice : choice + 1] == iota((ROWS, EXPERTS), 1)).astype(F32)
    earlier = (iota((ROWS, ROWS), 0) > iota((ROWS, ROWS), 1)).astype(BF16)
    before = dot(earlier, named.astype(BF16))
    return jnp.where(named > 0, before, -1.0)


def dispatch_kernel(latents, gain, ids, out, stacked, slots):
    at_group = pl.program_id(0)

    @pl.when(at_group == 0)
    def _():
        wide = latents[...].astype(F32)
        factor = lax.rsqrt(jnp.mean(wide * wide, axis=1, keepdims=True) + EPSILON)
        normed = (wide * factor * gain[...]).astype(BF16)
        stacked[:ROWS, :] = normed[:, :CHUNK]
        stacked[ROWS:, :] = normed[:, CHUNK:]
        slots[...] = slot_table(ids).astype(BF16)

    row = iota((GROUP_ROWS, 1), 0)
    expert_of = over_56(row)
    slot_of = row - over_28(row) * CAPACITY
    half_of = over_28(row) - expert_of * HALVES
    pick = (iota((GROUP_ROWS, EXPERTS), 1) == expert_of + at_group * GROUP).astype(BF16)
    match = dot_t(pick, slots[...]) == slot_of.astype(F32)
    chosen = jnp.concatenate(
        [jnp.where(match & (half_of == half), 1.0, 0.0) for half in range(HALVES)], axis=1
    )
    out[...] = dot(chosen.astype(BF16), stacked[...]).astype(BF16)


def dispatch(latents, gain, ids):
    return pl.pallas_call(
        dispatch_kernel,
        grid=(GROUPS,),
        in_specs=[
            pl.BlockSpec((ROWS, WIDTH), lambda i: (0, 0)),
            pl.BlockSpec((1, WIDTH), lambda i: (0, 0)),
            pl.BlockSpec((ROWS, TOP), lambda i: (0, 0)),
        ],
        out_specs=pl.BlockSpec((GROUP_ROWS, CHUNK), lambda i: (i, 0)),
        out_shape=jax.ShapeDtypeStruct((EXPERTS * BLOCK, CHUNK), BF16),
        scratch_shapes=[
            pltpu.VMEM((HALVES * ROWS, CHUNK), BF16),
            pltpu.VMEM((ROWS, EXPERTS), BF16),
        ],
        compiler_params=pltpu.CompilerParams(vmem_limit_bytes=VMEM_LIMIT),
        cost_estimate=pl.CostEstimate(
            flops=1_200_000_000, bytes_accessed=6_000_000, transcendentals=0
        ),
    )(latents, gain, ids)


def spread_rows():
    row = iota((SMALL_ROWS, SMALL_ROWS), 0)
    half = (row >= SMALL_SLOTS).astype(jnp.int32)
    slots = row - half * SMALL_SLOTS
    target = row - half * SMALL_SLOTS + over_28(slots) * CAPACITY + half * CAPACITY
    return (iota((SMALL_ROWS, SMALL_ROWS), 1) == target).astype(BF16)


def gathered_rows():
    row = iota((SMALL_ROWS, SMALL_ROWS), 0)
    block = over_56(row)
    half = over_28(row) - block * HALVES
    slot = row - over_28(row) * CAPACITY
    target = half * SMALL_SLOTS + block * CAPACITY + slot
    return (iota((SMALL_ROWS, SMALL_ROWS), 1) == target).astype(BF16)


HALF = SLOTS // 2


def whole_block(shape):
    return pl.BlockSpec(shape, lambda i: (0, 0))


def open_kernel(blocks, rows):
    order = spread_rows()
    for part in range(GROUP // SMALL):
        at, to = part * SMALL_ROWS, part * SMALL_SLOTS
        found = dot(order, blocks[at : at + SMALL_ROWS, :]).astype(BF16)
        rows[to : to + SMALL_SLOTS, :CHUNK] = found[:SMALL_SLOTS, :]
        rows[to : to + SMALL_SLOTS, CHUNK:] = found[SMALL_SLOTS:, :]


def opened(received):
    return pl.pallas_call(
        open_kernel,
        grid=(GROUPS,),
        in_specs=[pl.BlockSpec((GROUP_ROWS, CHUNK), lambda i: (i, 0))],
        out_specs=pl.BlockSpec((GROUP_ROWS // HALVES, WIDTH), lambda i: (i, 0)),
        out_shape=jax.ShapeDtypeStruct((SLOTS, WIDTH), BF16),
        compiler_params=pltpu.CompilerParams(vmem_limit_bytes=VMEM_LIMIT),
        cost_estimate=pl.CostEstimate(
            flops=1_000_000_000, bytes_accessed=9_000_000, transcendentals=0
        ),
    )(received)


def close_rows(order, rows, out):
    width = rows.shape[1] // 2
    for group in range(HALF // SMALL_SLOTS):
        taken = rows[group * SMALL_SLOTS : (group + 1) * SMALL_SLOTS, :]
        taken = jnp.concatenate([taken[:, :width], taken[:, width:]], axis=0)
        out[group * SMALL_ROWS : (group + 1) * SMALL_ROWS, :] = dot(order, taken).astype(BF16)


def side_by_side(left, right):
    return jnp.concatenate([left.astype(F32), right.astype(F32)], axis=1).astype(BF16)


def right_side(block):
    return pltpu.roll(block.astype(F32), REST, 1)[:, :REST].astype(BF16)


def pack_kernel(gate, up, down, first, second):
    first[:SHARD, :] = gate[:, :MAIN]
    first[SHARD : 2 * SHARD, :] = up[:, :MAIN]
    first[2 * SHARD : FIRST_MAIN, :] = down[: SPLIT[0], :MAIN]
    rest = side_by_side(gate[:, MAIN:], up[:, MAIN:])
    for block in range(SHARD // FIRST_REST):
        first[FIRST_MAIN:, block * 128 : (block + 1) * 128] = rest[
            block * FIRST_REST : (block + 1) * FIRST_REST, :
        ]
    first[FIRST_MAIN:, MAIN - 128 :] = side_by_side(
        down[:FIRST_REST, MAIN:], down[FIRST_REST : SPLIT[0], MAIN:]
    )
    second[: SPLIT[1], :] = down[SPLIT[0] :, :MAIN]
    middle = SPLIT[0] + SPLIT[1] // 2
    rest = side_by_side(down[SPLIT[0] : middle, MAIN:], down[middle:, MAIN:])
    for block in range(MAIN // 128):
        second[SPLIT[1] :, block * 128 : (block + 1) * 128] = rest[
            block * SECOND_REST : (block + 1) * SECOND_REST, :
        ]


def packed(gate, up, down):
    vmem = pl.BlockSpec(memory_space=pltpu.VMEM)
    return pl.pallas_call(
        pack_kernel,
        out_shape=(
            jax.ShapeDtypeStruct((FIRST_ROWS, MAIN), BF16),
            jax.ShapeDtypeStruct((SECOND_ROWS, MAIN), BF16),
        ),
        in_specs=[vmem] * 3,
        out_specs=(vmem, vmem),
        compiler_params=pltpu.CompilerParams(vmem_limit_bytes=VMEM_LIMIT),
        cost_estimate=pl.CostEstimate(flops=0, bytes_accessed=3_200_000, transcendentals=0),
    )(gate, up, down)


def expert_kernel(
    rows, gathered, hidden, out,
    taken, full, rests, blocks, down, down_rest, gates, outs, sems, out_sems,
):
    row_copies = [
        pltpu.make_async_copy(
            rows.at[pl.ds(half * HALF, HALF), :],
            taken.at[pl.ds(half * HALF, HALF), :],
            sems.at[half],
        )
        for half in range(2)
    ]
    gate_copies, up_copies, rest_copies = [], [], []
    for shard in range(N_DP):
        start = shard * FIRST_ROWS
        for which, copies in enumerate((gate_copies, up_copies)):
            copies.append(
                pltpu.make_async_copy(
                    gathered.at[pl.ds(start + which * SHARD, SHARD), :],
                    full.at[which, pl.ds(shard * SHARD, SHARD), :],
                    sems.at[2 + 4 * shard + which],
                )
            )
        rest_copies.append(
            pltpu.make_async_copy(
                gathered.at[pl.ds(start + FIRST_MAIN, FIRST_REST), :],
                blocks.at[shard],
                sems.at[2 + 4 * shard + 2],
            )
        )
        rest_copies.append(
            pltpu.make_async_copy(
                gathered.at[pl.ds(start + 2 * SHARD, SPLIT[0]), :],
                down.at[pl.ds(shard * SPLIT[0], SPLIT[0]), :],
                sems.at[2 + 4 * shard + 3],
            )
        )
    for copy in [row_copies[0]] + gate_copies + [row_copies[1]] + up_copies + rest_copies:
        copy.start()
    for copy in [row_copies[0]] + gate_copies:
        copy.wait()
    gates[:HALF, :] = dot(taken[:HALF, :], full[0])
    row_copies[1].wait()
    gates[HALF:, :] = dot(taken[HALF:, :], full[0])
    for copy in up_copies + rest_copies:
        copy.wait()
    for shard in range(N_DP):
        for block in range(SHARD // FIRST_REST):
            at = shard * SHARD + block * FIRST_REST
            rests[at : at + FIRST_REST, :] = blocks[shard, :, block * 128 : (block + 1) * 128]
        last = blocks[shard, :, MAIN - 128 :]
        at = shard * SPLIT[0]
        down_rest[at : at + FIRST_REST, :] = last[:, :REST]
        down_rest[at + FIRST_REST : at + SPLIT[0], :] = right_side(last)
    for half in range(2):
        at = slice(half * HALF, (half + 1) * HALF)
        gate = gates[at, :]
        up = dot(taken[at, :], full[1])
        hidden[at, :MAIN] = (gate / (1.0 + jnp.exp(-gate)) * up).astype(BF16)
        both = dot(taken[at, :], rests[...])
        gate, up = both[:, :REST], pltpu.roll(both, REST, 1)[:, :REST]
        hidden[at, MAIN:] = (gate / (1.0 + jnp.exp(-gate)) * up).astype(BF16)
    order = gathered_rows()
    out_copies = []
    for half in range(2):
        at = slice(half * HALF, (half + 1) * HALF)
        result = dot_t(hidden[at, :MAIN], down[...]) + dot_t(hidden[at, MAIN:], down_rest[...])
        close_rows(order, result.astype(BF16), outs.at[half])
        copy = pltpu.make_async_copy(
            outs.at[half],
            out.at[pl.ds(half * HALF * HALVES, HALF * HALVES), :],
            out_sems.at[half],
        )
        copy.start()
        out_copies.append(copy)
    for copy in out_copies:
        copy.wait()


def experts(rows, gathered):
    columns = N_DP * SPLIT[0]
    hbm = pl.BlockSpec(memory_space=pltpu.HBM)
    return pl.pallas_call(
        expert_kernel,
        out_shape=(
            jax.ShapeDtypeStruct((SLOTS, HID), BF16),
            jax.ShapeDtypeStruct((EXPERTS * BLOCK, columns // 2), BF16),
        ),
        in_specs=[hbm, hbm],
        out_specs=(pl.BlockSpec(memory_space=pltpu.VMEM), hbm),
        scratch_shapes=[
            pltpu.VMEM((SLOTS, WIDTH), BF16),
            pltpu.VMEM((2, WIDTH, MAIN), BF16),
            pltpu.VMEM((WIDTH, 2 * REST), BF16),
            pltpu.VMEM((N_DP, FIRST_REST, MAIN), BF16),
            pltpu.VMEM((columns, MAIN), BF16),
            pltpu.VMEM((columns, REST), BF16),
            pltpu.VMEM((SLOTS, MAIN), F32),
            pltpu.VMEM((2, HALF * HALVES, columns // 2), BF16),
            pltpu.SemaphoreType.DMA((2 + 4 * N_DP,)),
            pltpu.SemaphoreType.DMA((2,)),
        ],
        compiler_params=pltpu.CompilerParams(vmem_limit_bytes=VMEM_LIMIT),
        cost_estimate=pl.CostEstimate(
            flops=10_000_000_000, bytes_accessed=20_000_000, transcendentals=745_472
        ),
    )(rows, gathered)


def result_kernel(hidden, gathered, out, units, full, rest, blocks, outs, sems, out_sems):
    unit_copies = [
        pltpu.make_async_copy(
            hidden.at[pl.ds(half * HALF, HALF), :],
            units.at[pl.ds(half * HALF, HALF), :],
            sems.at[2 * N_DP + half],
        )
        for half in range(2)
    ]
    copies, rest_copies = [], []
    for shard in range(N_DP):
        start = shard * SECOND_ROWS
        copies.append(
            pltpu.make_async_copy(
                gathered.at[pl.ds(start, SPLIT[1]), :],
                full.at[pl.ds(shard * SPLIT[1], SPLIT[1]), :],
                sems.at[2 * shard],
            )
        )
        rest_copies.append(
            pltpu.make_async_copy(
                gathered.at[pl.ds(start + SPLIT[1], SECOND_REST), :],
                blocks.at[shard],
                sems.at[2 * shard + 1],
            )
        )
    for copy in rest_copies + [unit_copies[0]] + copies + [unit_copies[1]]:
        copy.start()
    for copy in rest_copies:
        copy.wait()
    for shard in range(N_DP):
        for block in range(MAIN // 128):
            at = shard * SPLIT[1] + block * SECOND_REST
            middle = at + SPLIT[1] // 2
            both = blocks[shard, :, block * 128 : (block + 1) * 128]
            rest[at : at + SECOND_REST, :] = both[:, :REST]
            rest[middle : middle + SECOND_REST, :] = right_side(both)
    for copy in [unit_copies[0]] + copies:
        copy.wait()
    order = gathered_rows()
    out_copies = []
    for half in range(2):
        if half == 1:
            unit_copies[1].wait()
        at = slice(half * HALF, (half + 1) * HALF)
        result = dot_t(units[at, :MAIN], full[...]) + dot_t(units[at, MAIN:], rest[...])
        close_rows(order, result.astype(BF16), outs.at[half])
        copy = pltpu.make_async_copy(
            outs.at[half],
            out.at[pl.ds(half * HALF * HALVES, HALF * HALVES), :],
            out_sems.at[half],
        )
        copy.start()
        out_copies.append(copy)
    for copy in out_copies:
        copy.wait()


def results(hidden, gathered):
    columns = N_DP * SPLIT[1]
    hbm = pl.BlockSpec(memory_space=pltpu.HBM)
    return pl.pallas_call(
        result_kernel,
        out_shape=jax.ShapeDtypeStruct((EXPERTS * BLOCK, columns // 2), BF16),
        in_specs=[hbm, hbm],
        out_specs=hbm,
        scratch_shapes=[
            pltpu.VMEM((SLOTS, HID), BF16),
            pltpu.VMEM((columns, MAIN), BF16),
            pltpu.VMEM((columns, REST), BF16),
            pltpu.VMEM((N_DP, SECOND_REST, MAIN), BF16),
            pltpu.VMEM((2, HALF * HALVES, columns // 2), BF16),
            pltpu.SemaphoreType.DMA((2 * N_DP + 2,)),
            pltpu.SemaphoreType.DMA((2,)),
        ],
        compiler_params=pltpu.CompilerParams(vmem_limit_bytes=VMEM_LIMIT),
        cost_estimate=pl.CostEstimate(
            flops=3_000_000_000, bytes_accessed=8_000_000, transcendentals=0
        ),
    )(hidden, gathered)


TERMS = 2
SHARE_ROWS = TERMS * HALVES * ROWS


def share_kernel(ids, weights, out, slots, terms):
    at_group = pl.program_id(0)

    @pl.when(at_group == 0)
    def _():
        slots[...] = slot_table(ids).astype(BF16)
        shares = jnp.zeros((ROWS, EXPERTS), F32)
        for choice in range(TOP):
            named = ids[:, choice : choice + 1] == iota((ROWS, EXPERTS), 1)
            shares = shares + jnp.where(named, weights[:, choice : choice + 1], 0.0)
        high = shares.astype(BF16)
        terms[:ROWS, :] = high
        terms[ROWS:, :] = (shares - high.astype(F32)).astype(BF16)

    row = iota((EXPERTS, GROUP_ROWS), 1)
    pick = (over_56(row) + at_group * GROUP == iota((EXPERTS, GROUP_ROWS), 0)).astype(BF16)
    lane = iota((ROWS, GROUP_ROWS), 1)
    slot_of = lane - over_28(lane) * CAPACITY
    half_of = over_28(lane) - over_56(lane) * HALVES
    match = dot(slots[...], pick) == slot_of.astype(F32)
    shares = dot(terms[...], pick)
    for term in range(TERMS):
        for half in range(HALVES):
            at = (term * HALVES + half) * ROWS
            out[at : at + ROWS, :] = jnp.where(
                match & (half_of == half), shares[term * ROWS : (term + 1) * ROWS], 0.0
            ).astype(BF16)


def share_table(ids, weights):
    return pl.pallas_call(
        share_kernel,
        grid=(GROUPS,),
        in_specs=[whole_block((ROWS, TOP)), whole_block((ROWS, TOP))],
        out_specs=pl.BlockSpec((SHARE_ROWS, GROUP_ROWS), lambda i: (i, 0)),
        out_shape=jax.ShapeDtypeStruct((GROUPS * SHARE_ROWS, GROUP_ROWS), BF16),
        scratch_shapes=[
            pltpu.VMEM((ROWS, EXPERTS), BF16),
            pltpu.VMEM((TERMS * ROWS, EXPERTS), BF16),
        ],
        compiler_params=pltpu.CompilerParams(vmem_limit_bytes=VMEM_LIMIT),
        cost_estimate=pl.CostEstimate(
            flops=50_000_000, bytes_accessed=2_000_000, transcendentals=0
        ),
    )(ids, weights)


def mix_blocks(shares, returned, table, blocks, total, sems):
    share_copies = [
        pltpu.make_async_copy(
            shares.at[pl.ds(g * SHARE_ROWS, SHARE_ROWS), :],
            table.at[pl.ds(g * SHARE_ROWS, SHARE_ROWS), :],
            sems.at[g],
        )
        for g in range(GROUPS)
    ]
    copies = [
        pltpu.make_async_copy(
            returned.at[pl.ds(g * GROUP_ROWS, GROUP_ROWS), :],
            blocks.at[pl.ds(g * GROUP_ROWS, GROUP_ROWS), :],
            sems.at[GROUPS + g],
        )
        for g in range(GROUPS)
    ]
    for g in range(GROUPS):
        share_copies[g].start()
        copies[g].start()
    step = HALVES * ROWS
    for g in range(GROUPS):
        share_copies[g].wait()
        copies[g].wait()
        found = dot(
            table[g * SHARE_ROWS : (g + 1) * SHARE_ROWS, :],
            blocks[g * GROUP_ROWS : (g + 1) * GROUP_ROWS, :],
        )
        found = found[:step] + found[step:]
        total[...] = found if g == 0 else total[...] + found


def mix_kernel(shares, returned, out, table, blocks, total, sems):
    mix_blocks(shares, returned, table, blocks, total, sems)
    width = returned.shape[1]
    out[:, :width] = total[:ROWS, :]
    out[:, width:] = total[ROWS:, :]


def last_kernel(shares, returned, first, latents, out, table, blocks, total, sems):
    mix_blocks(shares, returned, table, blocks, total, sems)
    pieces = []
    for shard in range(N_DP):
        half, at = shard // 4, shard % 4 * SPLIT[1]
        pieces.append(first[:, shard * SPLIT[0] : (shard + 1) * SPLIT[0]])
        pieces.append(total[half * ROWS : (half + 1) * ROWS, at : at + SPLIT[1]])
    whole = jnp.concatenate(pieces, axis=1)
    out[...] = (latents[...].astype(F32) + whole).astype(BF16)


def mixed(shares, returned, *last):
    width = returned.shape[1]
    hbm = pl.BlockSpec(memory_space=pl.ANY if last else pltpu.HBM)
    vmem = pl.BlockSpec(memory_space=pltpu.VMEM)
    out, kernel = jax.ShapeDtypeStruct((ROWS, 2 * width), F32), mix_kernel
    if last:
        out, kernel = jax.ShapeDtypeStruct((ROWS, WIDTH), BF16), last_kernel
    return pl.pallas_call(
        kernel,
        in_specs=[hbm, hbm] + [vmem] * len(last),
        out_shape=out,
        out_specs=vmem,
        scratch_shapes=[
            pltpu.VMEM(shares.shape, BF16),
            pltpu.VMEM(returned.shape, BF16),
            pltpu.VMEM((HALVES * ROWS, width), F32),
            pltpu.SemaphoreType.DMA((2 * GROUPS,)),
        ],
        compiler_params=pltpu.CompilerParams(vmem_limit_bytes=24 * 1024 * 1024),
        cost_estimate=pl.CostEstimate(
            flops=1_200_000_000, bytes_accessed=4_000_000, transcendentals=0
        ),
    )(shares, returned, *last)


SAME_CORE = [list(range(core, EXPERTS, 2)) for core in range(2)]


def other_core(value):
    return lax.ppermute(value, "expert", [(at, at ^ 1) for at in range(EXPERTS)])


def between_chips(pieces):
    return lax.all_to_all(
        pieces,
        "expert",
        split_axis=0,
        concat_axis=0,
        tiled=True,
        axis_index_groups=SAME_CORE,
    )


def scattered(part):
    pieces = between_chips(part.reshape(EXPERTS // 2, -1, WIDTH))
    return jnp.sum(pieces.astype(F32), axis=0)


def exchange_sum(total, bit):
    return total + lax.ppermute(total, "dp", [(at, at ^ bit) for at in range(N_DP)])


def spread(total):
    pieces = jnp.broadcast_to(total.astype(BF16), (EXPERTS // 2,) + total.shape)
    return between_chips(pieces).reshape(-1, WIDTH)


def both_halves(half):
    far_half = other_core(half)
    low = lax.axis_index("expert") % 2 == 0
    whole = jnp.concatenate(
        [jnp.where(low, half, far_half), jnp.where(low, far_half, half)], axis=0
    )
    return whole.astype(F32)


def exchanged(blocks):
    rows, columns = blocks.shape
    return lax.all_to_all(
        blocks.reshape(EXPERTS, rows // EXPERTS, columns),
        "expert",
        split_axis=0,
        concat_axis=0,
        tiled=True,
    ).reshape(rows, columns)


def tied(*values):
    return lax.optimization_barrier(values)


def per_device(
    queries,
    patch_keys,
    patch_values,
    norm_gain,
    gate_weight,
    up_weight,
    down_weight,
    expert_ids,
    combine_weights,
    latent_grad,
):
    parity = lax.axis_index("expert") % 2
    which = parity.reshape(1).astype(jnp.int32)
    far_keys, far_values = other_core(patch_keys), other_core(patch_values)
    shard, second_shard = packed(gate_weight[0], up_weight[0], down_weight[0].T)
    gathered = lax.all_gather(shard, "dp", axis=0, tiled=True)
    patches = (which, queries, patch_keys, far_keys, patch_values, far_values)
    latents, grad_part = attention(*patches, latent_grad)
    latents, second_shard = tied(latents, second_shard)
    second_gathered = lax.all_gather(second_shard, "dp", axis=0, tiled=True)
    total = scattered(grad_part)
    sent = dispatch(latents, norm_gain.reshape(1, WIDTH), expert_ids)
    sent, total, same_ids = tied(sent, total, expert_ids)
    received = exchanged(sent)
    shares = share_table(same_ids, combine_weights)
    total = exchange_sum(exchange_sum(exchange_sum(total, 1), 2), 4)
    received, total, shares = tied(received, total, shares)
    rows = opened(received)
    rows, total = tied(rows, total)
    half = spread(total)
    hidden, first = experts(rows, gathered)
    hidden, first, half = tied(hidden, first, half)
    first = exchanged(first)
    second = exchanged(results(hidden, second_gathered))
    first_mix = mixed(shares, first)
    layer_out = mixed(shares, second, first_mix, latents)
    query_grad = both_halves(half)
    return (layer_out, query_grad)


def solution(mesh):
    return jax.shard_map(
        per_device,
        mesh=mesh,
        in_specs=(
            P(),
            P(("dp", "expert"), None),
            P(("dp", "expert"), None),
            P(),
            P("expert", "dp", None),
            P("expert", "dp", None),
            P("expert", None, "dp"),
            P(("dp", "expert"), None),
            P(("dp", "expert"), None),
            P(("dp", "expert"), None),
        ),
        out_specs=(P(("dp", "expert"), None), P()),
        check_vma=False,
    )
```

```python
import functools
import math

import jax
import jax.numpy as jnp
from jax import lax
from jax.experimental import pallas as pl
from jax.experimental.pallas import tpu as pltpu
from jax.sharding import PartitionSpec as P

HEADS = 20
HEAD_DIM = 128
WIDTH = HEADS * HEAD_DIM
ROWS = 128
PATCHES = 512
TOP = 6
EXPERTS = 32
HID = 832
CAPACITY = 28
N_DP = 8
SHARD = WIDTH // N_DP
HALVES = 2
BLOCK = HALVES * CAPACITY
GROUP = 8
GROUPS = EXPERTS // GROUP
GROUP_ROWS = GROUP * BLOCK
SMALL = 4
SMALL_ROWS = SMALL * BLOCK
SMALL_SLOTS = SMALL * CAPACITY
SLOTS = EXPERTS * CAPACITY
CHUNK = WIDTH // 2
SPLIT = (128, SHARD - 128)
MAIN = 768
REST = HID - MAIN
FIRST_MAIN = 2 * SHARD + SPLIT[0]
FIRST_REST = 64
FIRST_ROWS = FIRST_MAIN + FIRST_REST
SECOND_REST = 16
SECOND_ROWS = SPLIT[1] + SECOND_REST
EPSILON = 1e-06
SCALE = 1.0 / math.sqrt(HEAD_DIM)
HEADS_PER_STEP = 4
VMEM_LIMIT = 56 * 1024 * 1024

F32 = jnp.float32
BF16 = jnp.bfloat16


def dot(a, b):
    return jnp.dot(a, b, preferred_element_type=F32)


def dot_t(a, b):
    return lax.dot_general(a, b, (((1,), (1,)), ((), ())), preferred_element_type=F32)


def iota(shape, axis):
    return lax.broadcasted_iota(jnp.int32, shape, axis)


def over_28(value):
    return (value * 1171) >> 15


def over_56(value):
    return (value * 1171) >> 16


def head_weights(queries, near_keys, far_keys):
    near = dot_t(queries, near_keys) * SCALE
    far = dot_t(queries, far_keys) * SCALE
    peak = jnp.maximum(
        jnp.max(near, axis=1, keepdims=True), jnp.max(far, axis=1, keepdims=True)
    )
    near = jnp.exp(near - peak)
    far = jnp.exp(far - peak)
    total = jnp.sum(near, axis=1, keepdims=True) + jnp.sum(far, axis=1, keepdims=True)
    inverse = 1.0 / total
    return near * inverse, far * inverse


def attention_kernel(
    parity, queries, near_keys, far_keys, near_values, far_values, cotangent, latents, grad
):
    for head in range(HEADS_PER_STEP):
        at = slice(head * HEAD_DIM, (head + 1) * HEAD_DIM)
        near, far = head_weights(queries[:, at], near_keys[:, at], far_keys[:, at])
        attended = dot(near.astype(BF16), near_values[:, at]) + dot(
            far.astype(BF16), far_values[:, at]
        )
        rounded = attended.astype(BF16)
        latents[:, at] = rounded
        given = cotangent[:, at]
        inner = jnp.sum(given.astype(F32) * rounded.astype(F32), axis=1, keepdims=True)
        near = near * (dot_t(given, near_values[:, at]) - inner) * SCALE
        far = far * (dot_t(given, far_values[:, at]) - inner) * SCALE
        part = dot(near.astype(BF16), near_keys[:, at]) + dot(far.astype(BF16), far_keys[:, at])
        grad[:, at] = part.astype(BF16)


def attention(parity, queries, keys, far_keys, values, far_values, cotangent):
    wide = HEADS_PER_STEP * HEAD_DIM
    own = pl.BlockSpec((ROWS, wide), lambda i, parity: (0, i))
    patches = pl.BlockSpec((PATCHES, wide), lambda i, parity: (0, i))
    asked = pl.BlockSpec((ROWS, wide), lambda i, parity: (parity[0], i))
    return pl.pallas_call(
        attention_kernel,
        out_shape=(
            jax.ShapeDtypeStruct((ROWS, WIDTH), BF16),
            jax.ShapeDtypeStruct((ROWS, WIDTH), BF16),
        ),
        grid_spec=pltpu.PrefetchScalarGridSpec(
            num_scalar_prefetch=1,
            grid=(HEADS // HEADS_PER_STEP,),
            in_specs=[asked, patches, patches, patches, patches, own],
            out_specs=(own, own),
        ),
        compiler_params=pltpu.CompilerParams(vmem_limit_bytes=VMEM_LIMIT),
        cost_estimate=pl.CostEstimate(
            flops=2_684_354_560, bytes_accessed=13_000_000, transcendentals=2_621_440
        ),
    )(parity, queries, keys, far_keys, values, far_values, cotangent)


def slot_table(ids):
    named = jnp.zeros((ROWS, EXPERTS), F32)
    for choice in range(TOP):
        named = named + (ids[:, choice : choice + 1] == iota((ROWS, EXPERTS), 1)).astype(F32)
    earlier = (iota((ROWS, ROWS), 0) > iota((ROWS, ROWS), 1)).astype(BF16)
    before = dot(earlier, named.astype(BF16))
    return jnp.where(named > 0, before, -1.0)


def dispatch_kernel(latents, gain, ids, out, stacked, slots):
    at_group = pl.program_id(0)

    @pl.when(at_group == 0)
    def _():
        wide = latents[...].astype(F32)
        factor = lax.rsqrt(jnp.mean(wide * wide, axis=1, keepdims=True) + EPSILON)
        normed = (wide * factor * gain[...]).astype(BF16)
        stacked[:ROWS, :] = normed[:, :CHUNK]
        stacked[ROWS:, :] = normed[:, CHUNK:]
        slots[...] = slot_table(ids).astype(BF16)

    row = iota((GROUP_ROWS, 1), 0)
    expert_of = over_56(row)
    slot_of = row - over_28(row) * CAPACITY
    half_of = over_28(row) - expert_of * HALVES
    pick = (iota((GROUP_ROWS, EXPERTS), 1) == expert_of + at_group * GROUP).astype(BF16)
    match = dot_t(pick, slots[...]) == slot_of.astype(F32)
    chosen = jnp.concatenate(
        [jnp.where(match & (half_of == half), 1.0, 0.0) for half in range(HALVES)], axis=1
    )
    out[...] = dot(chosen.astype(BF16), stacked[...]).astype(BF16)


def dispatch(latents, gain, ids):
    return pl.pallas_call(
        dispatch_kernel,
        grid=(GROUPS,),
        in_specs=[
            pl.BlockSpec((ROWS, WIDTH), lambda i: (0, 0)),
            pl.BlockSpec((1, WIDTH), lambda i: (0, 0)),
            pl.BlockSpec((ROWS, TOP), lambda i: (0, 0)),
        ],
        out_specs=pl.BlockSpec((GROUP_ROWS, CHUNK), lambda i: (i, 0)),
        out_shape=jax.ShapeDtypeStruct((EXPERTS * BLOCK, CHUNK), BF16),
        scratch_shapes=[
            pltpu.VMEM((HALVES * ROWS, CHUNK), BF16),
            pltpu.VMEM((ROWS, EXPERTS), BF16),
        ],
        compiler_params=pltpu.CompilerParams(vmem_limit_bytes=VMEM_LIMIT),
        cost_estimate=pl.CostEstimate(
            flops=1_200_000_000, bytes_accessed=6_000_000, transcendentals=0
        ),
    )(latents, gain, ids)


HALF = SLOTS // 2


def whole_block(shape):
    return pl.BlockSpec(shape, lambda i: (0, 0))


def open_kernel(blocks, rows):
    for part in range(GROUP // SMALL):
        at, to = part * SMALL_ROWS, part * SMALL_SLOTS
        taken = blocks[at : at + SMALL_ROWS, :].astype(F32)
        for half in range(HALVES):
            pieces = [
                taken[block * BLOCK + half * CAPACITY : block * BLOCK + (half + 1) * CAPACITY, :]
                for block in range(SMALL)
            ]
            rows[to : to + SMALL_SLOTS, half * CHUNK : (half + 1) * CHUNK] = jnp.concatenate(
                pieces, axis=0
            ).astype(BF16)


def opened(received):
    return pl.pallas_call(
        open_kernel,
        grid=(GROUPS,),
        in_specs=[pl.BlockSpec((GROUP_ROWS, CHUNK), lambda i: (i, 0))],
        out_specs=pl.BlockSpec((GROUP_ROWS // HALVES, WIDTH), lambda i: (i, 0)),
        out_shape=jax.ShapeDtypeStruct((SLOTS, WIDTH), BF16),
        compiler_params=pltpu.CompilerParams(vmem_limit_bytes=VMEM_LIMIT),
        cost_estimate=pl.CostEstimate(
            flops=1_000_000_000, bytes_accessed=9_000_000, transcendentals=0
        ),
    )(received)


def close_rows(rows, out):
    width = rows.shape[1] // 2
    for pair in range(HALF // CAPACITY // 2):
        pieces = []
        for block in (2 * pair, 2 * pair + 1):
            taken = rows[block * CAPACITY : (block + 1) * CAPACITY, :]
            pieces += [taken[:, :width], taken[:, width:]]
        at = 2 * pair * BLOCK
        out[at : at + 2 * BLOCK, :] = jnp.concatenate(pieces, axis=0).astype(BF16)


def side_by_side(left, right):
    return jnp.concatenate([left.astype(F32), right.astype(F32)], axis=1).astype(BF16)


def right_side(block):
    return pltpu.roll(block.astype(F32), REST, 1)[:, :REST].astype(BF16)


def pack_kernel(
    gate, up, down, first, second, gates, ups, downs, first_rest, second_rest, sems, out_sems
):
    loads = [
        pltpu.make_async_copy(source, target, sems.at[index])
        for index, (source, target) in enumerate(((gate, gates), (up, ups), (down, downs)))
    ]
    for load in loads:
        load.start()
    outs = []

    def send(source, target):
        outs.append(pltpu.make_async_copy(source, target, out_sems.at[len(outs)]))
        outs[-1].start()

    main = pl.ds(0, MAIN)
    loads[0].wait()
    send(gates.at[:, main], first.at[pl.ds(0, SHARD), :])
    loads[1].wait()
    send(ups.at[:, main], first.at[pl.ds(SHARD, SHARD), :])
    loads[2].wait()
    send(downs.at[pl.ds(0, SPLIT[0]), main], first.at[pl.ds(2 * SHARD, SPLIT[0]), :])
    send(downs.at[pl.ds(SPLIT[0], SPLIT[1]), main], second.at[pl.ds(0, SPLIT[1]), :])
    rest = side_by_side(gates[:, MAIN:], ups[:, MAIN:])
    for block in range(SHARD // FIRST_REST):
        first_rest[:, block * 128 : (block + 1) * 128] = rest[
            block * FIRST_REST : (block + 1) * FIRST_REST, :
        ]
    first_rest[:, MAIN - 128 :] = side_by_side(
        downs[:FIRST_REST, MAIN:], downs[FIRST_REST : SPLIT[0], MAIN:]
    )
    send(first_rest, first.at[pl.ds(FIRST_MAIN, FIRST_REST), :])
    middle = SPLIT[0] + SPLIT[1] // 2
    rest = side_by_side(downs[SPLIT[0] : middle, MAIN:], downs[middle:, MAIN:])
    for block in range(MAIN // 128):
        second_rest[:, block * 128 : (block + 1) * 128] = rest[
            block * SECOND_REST : (block + 1) * SECOND_REST, :
        ]
    send(second_rest, second.at[pl.ds(SPLIT[1], SECOND_REST), :])
    for out in outs:
        out.wait()


def packed(gate, up, down):
    hbm = pl.BlockSpec(memory_space=pltpu.HBM)
    return pl.pallas_call(
        pack_kernel,
        out_shape=(
            jax.ShapeDtypeStruct((FIRST_ROWS, MAIN), BF16),
            jax.ShapeDtypeStruct((SECOND_ROWS, MAIN), BF16),
        ),
        in_specs=[hbm] * 3,
        out_specs=(hbm, hbm),
        scratch_shapes=[pltpu.VMEM((SHARD, HID), BF16)] * 3
        + [
            pltpu.VMEM((FIRST_REST, MAIN), BF16),
            pltpu.VMEM((SECOND_REST, MAIN), BF16),
            pltpu.SemaphoreType.DMA((3,)),
            pltpu.SemaphoreType.DMA((6,)),
        ],
        compiler_params=pltpu.CompilerParams(vmem_limit_bytes=VMEM_LIMIT),
        cost_estimate=pl.CostEstimate(flops=0, bytes_accessed=3_200_000, transcendentals=0),
    )(gate, up, down)


def expert_kernel(
    rows, gathered, hidden, out,
    taken, full, rests, blocks, down, down_rest, gates, outs, sems, out_sems,
):
    row_copies = [
        pltpu.make_async_copy(
            rows.at[pl.ds(half * HALF, HALF), :],
            taken.at[pl.ds(half * HALF, HALF), :],
            sems.at[half],
        )
        for half in range(2)
    ]
    gate_copies, up_copies, rest_copies = [], [], []
    for shard in range(N_DP):
        start = shard * FIRST_ROWS
        for which, copies in enumerate((gate_copies, up_copies)):
            copies.append(
                pltpu.make_async_copy(
                    gathered.at[pl.ds(start + which * SHARD, SHARD), :],
                    full.at[which, pl.ds(shard * SHARD, SHARD), :],
                    sems.at[2 + 4 * shard + which],
                )
            )
        rest_copies.append(
            pltpu.make_async_copy(
                gathered.at[pl.ds(start + FIRST_MAIN, FIRST_REST), :],
                blocks.at[shard],
                sems.at[2 + 4 * shard + 2],
            )
        )
        rest_copies.append(
            pltpu.make_async_copy(
                gathered.at[pl.ds(start + 2 * SHARD, SPLIT[0]), :],
                down.at[pl.ds(shard * SPLIT[0], SPLIT[0]), :],
                sems.at[2 + 4 * shard + 3],
            )
        )
    for copy in [row_copies[0]] + gate_copies + [row_copies[1]] + up_copies + rest_copies:
        copy.start()
    for copy in [row_copies[0]] + gate_copies:
        copy.wait()
    gates[:HALF, :] = dot(taken[:HALF, :], full[0])
    row_copies[1].wait()
    gates[HALF:, :] = dot(taken[HALF:, :], full[0])
    for copy in up_copies + rest_copies:
        copy.wait()
    for shard in range(N_DP):
        for block in range(SHARD // FIRST_REST):
            at = shard * SHARD + block * FIRST_REST
            rests[at : at + FIRST_REST, :] = blocks[shard, :, block * 128 : (block + 1) * 128]
        last = blocks[shard, :, MAIN - 128 :]
        at = shard * SPLIT[0]
        down_rest[at : at + FIRST_REST, :] = last[:, :REST]
        down_rest[at + FIRST_REST : at + SPLIT[0], :] = right_side(last)
    gate = gates[...]
    up = dot(taken[...], full[1])
    hidden[:, :MAIN] = (gate / (1.0 + jnp.exp(-gate)) * up).astype(BF16)
    both = dot(taken[...], rests[...])
    gate, up = both[:, :REST], pltpu.roll(both, REST, 1)[:, :REST]
    hidden[:, MAIN:] = (gate / (1.0 + jnp.exp(-gate)) * up).astype(BF16)
    out_copies = []
    for half in range(2):
        at = slice(half * HALF, (half + 1) * HALF)
        result = dot_t(hidden[at, :MAIN], down[...]) + dot_t(hidden[at, MAIN:], down_rest[...])
        close_rows(result, outs.at[half])
        copy = pltpu.make_async_copy(
            outs.at[half],
            out.at[pl.ds(half * HALF * HALVES, HALF * HALVES), :],
            out_sems.at[half],
        )
        copy.start()
        out_copies.append(copy)
    for copy in out_copies:
        copy.wait()


def experts(rows, gathered):
    columns = N_DP * SPLIT[0]
    hbm = pl.BlockSpec(memory_space=pltpu.HBM)
    return pl.pallas_call(
        expert_kernel,
        out_shape=(
            jax.ShapeDtypeStruct((SLOTS, HID), BF16),
            jax.ShapeDtypeStruct((EXPERTS * BLOCK, columns // 2), BF16),
        ),
        in_specs=[hbm, hbm],
        out_specs=(pl.BlockSpec(memory_space=pltpu.VMEM), hbm),
        scratch_shapes=[
            pltpu.VMEM((SLOTS, WIDTH), BF16),
            pltpu.VMEM((2, WIDTH, MAIN), BF16),
            pltpu.VMEM((WIDTH, 2 * REST), BF16),
            pltpu.VMEM((N_DP, FIRST_REST, MAIN), BF16),
            pltpu.VMEM((columns, MAIN), BF16),
            pltpu.VMEM((columns, REST), BF16),
            pltpu.VMEM((SLOTS, MAIN), F32),
            pltpu.VMEM((2, HALF * HALVES, columns // 2), BF16),
            pltpu.SemaphoreType.DMA((2 + 4 * N_DP,)),
            pltpu.SemaphoreType.DMA((2,)),
        ],
        compiler_params=pltpu.CompilerParams(vmem_limit_bytes=VMEM_LIMIT),
        cost_estimate=pl.CostEstimate(
            flops=10_000_000_000, bytes_accessed=20_000_000, transcendentals=745_472
        ),
    )(rows, gathered)


def result_kernel(hidden, gathered, out, units, full, rest, blocks, outs, sems, out_sems):
    unit_copies = [
        pltpu.make_async_copy(
            hidden.at[pl.ds(half * HALF, HALF), :],
            units.at[pl.ds(half * HALF, HALF), :],
            sems.at[2 * N_DP + half],
        )
        for half in range(2)
    ]
    copies, rest_copies = [], []
    for shard in range(N_DP):
        start = shard * SECOND_ROWS
        copies.append(
            pltpu.make_async_copy(
                gathered.at[pl.ds(start, SPLIT[1]), :],
                full.at[pl.ds(shard * SPLIT[1], SPLIT[1]), :],
                sems.at[2 * shard],
            )
        )
        rest_copies.append(
            pltpu.make_async_copy(
                gathered.at[pl.ds(start + SPLIT[1], SECOND_REST), :],
                blocks.at[shard],
                sems.at[2 * shard + 1],
            )
        )
    for copy in rest_copies + [unit_copies[0]] + copies + [unit_copies[1]]:
        copy.start()
    for copy in rest_copies:
        copy.wait()
    for shard in range(N_DP):
        for block in range(MAIN // 128):
            at = shard * SPLIT[1] + block * SECOND_REST
            middle = at + SPLIT[1] // 2
            both = blocks[shard, :, block * 128 : (block + 1) * 128]
            rest[at : at + SECOND_REST, :] = both[:, :REST]
            rest[middle : middle + SECOND_REST, :] = right_side(both)
    for copy in [unit_copies[0]] + copies:
        copy.wait()
    out_copies = []
    for half in range(2):
        if half == 1:
            unit_copies[1].wait()
        at = slice(half * HALF, (half + 1) * HALF)
        result = dot_t(units[at, :MAIN], full[...]) + dot_t(units[at, MAIN:], rest[...])
        close_rows(result, outs.at[half])
        copy = pltpu.make_async_copy(
            outs.at[half],
            out.at[pl.ds(half * HALF * HALVES, HALF * HALVES), :],
            out_sems.at[half],
        )
        copy.start()
        out_copies.append(copy)
    for copy in out_copies:
        copy.wait()


def results(hidden, gathered):
    columns = N_DP * SPLIT[1]
    hbm = pl.BlockSpec(memory_space=pltpu.HBM)
    return pl.pallas_call(
        result_kernel,
        out_shape=jax.ShapeDtypeStruct((EXPERTS * BLOCK, columns // 2), BF16),
        in_specs=[hbm, hbm],
        out_specs=hbm,
        scratch_shapes=[
            pltpu.VMEM((SLOTS, HID), BF16),
            pltpu.VMEM((columns, MAIN), BF16),
            pltpu.VMEM((columns, REST), BF16),
            pltpu.VMEM((N_DP, SECOND_REST, MAIN), BF16),
            pltpu.VMEM((2, HALF * HALVES, columns // 2), BF16),
            pltpu.SemaphoreType.DMA((2 * N_DP + 2,)),
            pltpu.SemaphoreType.DMA((2,)),
        ],
        compiler_params=pltpu.CompilerParams(vmem_limit_bytes=63 * 1024 * 1024),
        cost_estimate=pl.CostEstimate(
            flops=3_000_000_000, bytes_accessed=8_000_000, transcendentals=0
        ),
    )(hidden, gathered)


TERMS = 2
SHARE_ROWS = TERMS * HALVES * ROWS


def share_kernel(ids, weights, total, out, repeated, slots, terms):
    at_group = pl.program_id(0)
    for copy in range(EXPERTS // 2 // GROUPS):
        repeated[copy] = total[...].astype(BF16)

    @pl.when(at_group == 0)
    def _():
        slots[...] = slot_table(ids).astype(BF16)
        shares = jnp.zeros((ROWS, EXPERTS), F32)
        for choice in range(TOP):
            named = ids[:, choice : choice + 1] == iota((ROWS, EXPERTS), 1)
            shares = shares + jnp.where(named, weights[:, choice : choice + 1], 0.0)
        high = shares.astype(BF16)
        terms[:ROWS, :] = high
        terms[ROWS:, :] = (shares - high.astype(F32)).astype(BF16)

    row = iota((EXPERTS, GROUP_ROWS), 1)
    pick = (over_56(row) + at_group * GROUP == iota((EXPERTS, GROUP_ROWS), 0)).astype(BF16)
    lane = iota((ROWS, GROUP_ROWS), 1)
    slot_of = lane - over_28(lane) * CAPACITY
    half_of = over_28(lane) - over_56(lane) * HALVES
    match = dot(slots[...], pick) == slot_of.astype(F32)
    shares = dot(terms[...], pick)
    for term in range(TERMS):
        for half in range(HALVES):
            at = (term * HALVES + half) * ROWS
            out[at : at + ROWS, :] = jnp.where(
                match & (half_of == half), shares[term * ROWS : (term + 1) * ROWS], 0.0
            ).astype(BF16)


def share_table(ids, weights, total):
    chips = EXPERTS // 2
    return pl.pallas_call(
        share_kernel,
        grid=(GROUPS,),
        in_specs=[
            whole_block((ROWS, TOP)),
            whole_block((ROWS, TOP)),
            whole_block(total.shape),
        ],
        out_specs=(
            pl.BlockSpec((SHARE_ROWS, GROUP_ROWS), lambda i: (i, 0)),
            pl.BlockSpec((chips // GROUPS,) + total.shape, lambda i: (i, 0, 0)),
        ),
        out_shape=(
            jax.ShapeDtypeStruct((GROUPS * SHARE_ROWS, GROUP_ROWS), BF16),
            jax.ShapeDtypeStruct((chips,) + total.shape, BF16),
        ),
        scratch_shapes=[
            pltpu.VMEM((ROWS, EXPERTS), BF16),
            pltpu.VMEM((TERMS * ROWS, EXPERTS), BF16),
        ],
        compiler_params=pltpu.CompilerParams(vmem_limit_bytes=VMEM_LIMIT),
        cost_estimate=pl.CostEstimate(
            flops=50_000_000, bytes_accessed=3_000_000, transcendentals=0
        ),
    )(ids, weights, total)


def mix_blocks(shares, returned, table, blocks, total, sems, later=()):
    share_copies = [
        pltpu.make_async_copy(
            shares.at[pl.ds(g * SHARE_ROWS, SHARE_ROWS), :],
            table.at[pl.ds(g * SHARE_ROWS, SHARE_ROWS), :],
            sems.at[g],
        )
        for g in range(GROUPS)
    ]
    copies = [
        pltpu.make_async_copy(
            returned.at[pl.ds(g * GROUP_ROWS, GROUP_ROWS), :],
            blocks.at[pl.ds(g * GROUP_ROWS, GROUP_ROWS), :],
            sems.at[GROUPS + g],
        )
        for g in range(GROUPS)
    ]
    for g in range(GROUPS):
        share_copies[g].start()
        copies[g].start()
    for copy in later:
        copy.start()
    step = HALVES * ROWS
    for g in range(GROUPS):
        share_copies[g].wait()
        copies[g].wait()
        found = dot(
            table[g * SHARE_ROWS : (g + 1) * SHARE_ROWS, :],
            blocks[g * GROUP_ROWS : (g + 1) * GROUP_ROWS, :],
        )
        found = found[:step] + found[step:]
        total[...] = found if g == 0 else total[...] + found
    for copy in later:
        copy.wait()


def mix_kernel(shares, returned, out, table, blocks, total, sems):
    mix_blocks(shares, returned, table, blocks, total, sems)
    width = returned.shape[1]
    out[:, :width] = total[:ROWS, :]
    out[:, width:] = total[ROWS:, :]


def last_kernel(
    shares, returned, first, latents, out, table, blocks, total, sems, others, own, last_sems
):
    copies = [
        pltpu.make_async_copy(first, others, last_sems.at[0]),
        pltpu.make_async_copy(latents, own, last_sems.at[1]),
    ]
    mix_blocks(shares, returned, table, blocks, total, sems, copies)
    pieces = []
    for shard in range(N_DP):
        half, at = shard // 4, shard % 4 * SPLIT[1]
        pieces.append(others[:, shard * SPLIT[0] : (shard + 1) * SPLIT[0]])
        pieces.append(total[half * ROWS : (half + 1) * ROWS, at : at + SPLIT[1]])
    whole = jnp.concatenate(pieces, axis=1)
    out[...] = (own[...].astype(F32) + whole).astype(BF16)


def mixed(shares, returned, *last):
    width = returned.shape[1]
    hbm = pl.BlockSpec(memory_space=pltpu.HBM)
    out, kernel = jax.ShapeDtypeStruct((ROWS, 2 * width), F32), mix_kernel
    scratch = [
        pltpu.VMEM(shares.shape, BF16),
        pltpu.VMEM(returned.shape, BF16),
        pltpu.VMEM((HALVES * ROWS, width), F32),
        pltpu.SemaphoreType.DMA((2 * GROUPS,)),
    ]
    if last:
        out, kernel = jax.ShapeDtypeStruct((ROWS, WIDTH), BF16), last_kernel
        scratch += [pltpu.VMEM(value.shape, value.dtype) for value in last]
        scratch += [pltpu.SemaphoreType.DMA((2,))]
    return pl.pallas_call(
        kernel,
        in_specs=[hbm] * (2 + len(last)),
        out_shape=out,
        out_specs=pl.BlockSpec(memory_space=pltpu.VMEM),
        scratch_shapes=scratch,
        compiler_params=pltpu.CompilerParams(vmem_limit_bytes=63 * 1024 * 1024),
        cost_estimate=pl.CostEstimate(
            flops=1_200_000_000, bytes_accessed=4_000_000, transcendentals=0
        ),
    )(shares, returned, *last)


SAME_CORE = [list(range(core, EXPERTS, 2)) for core in range(2)]


def other_core(value):
    return lax.ppermute(value, "expert", [(at, at ^ 1) for at in range(EXPERTS)])


def between_chips(pieces):
    return lax.all_to_all(
        pieces,
        "expert",
        split_axis=0,
        concat_axis=0,
        tiled=True,
        axis_index_groups=SAME_CORE,
    )


def scattered(part):
    pieces = between_chips(part.reshape(EXPERTS // 2, -1, WIDTH))
    return jnp.sum(pieces.astype(F32), axis=0)


def exchange_sum(total, bit):
    return total + lax.ppermute(total, "dp", [(at, at ^ bit) for at in range(N_DP)])


def both_halves(half):
    far_half = other_core(half)
    low = lax.axis_index("expert") % 2 == 0
    whole = jnp.concatenate(
        [jnp.where(low, half, far_half), jnp.where(low, far_half, half)], axis=0
    )
    return whole.astype(F32)


def exchanged(blocks):
    rows, columns = blocks.shape
    return lax.all_to_all(
        blocks.reshape(EXPERTS, rows // EXPERTS, columns),
        "expert",
        split_axis=0,
        concat_axis=0,
        tiled=True,
    ).reshape(rows, columns)


def tied(*values):
    return lax.optimization_barrier(values)


def per_device(
    queries,
    patch_keys,
    patch_values,
    norm_gain,
    gate_weight,
    up_weight,
    down_weight,
    expert_ids,
    combine_weights,
    latent_grad,
):
    parity = lax.axis_index("expert") % 2
    which = parity.reshape(1).astype(jnp.int32)
    far_keys, far_values = other_core(patch_keys), other_core(patch_values)
    shard, second_shard = packed(gate_weight[0], up_weight[0], down_weight[0].T)
    gathered = lax.all_gather(shard, "dp", axis=0, tiled=True)
    patches = (which, queries, patch_keys, far_keys, patch_values, far_values)
    latents, grad_part = attention(*patches, latent_grad)
    latents, second_shard = tied(latents, second_shard)
    second_gathered = lax.all_gather(second_shard, "dp", axis=0, tiled=True)
    total = scattered(grad_part)
    sent = dispatch(latents, norm_gain.reshape(1, WIDTH), expert_ids)
    sent, total, same_ids = tied(sent, total, expert_ids)
    received = exchanged(sent)
    total = exchange_sum(exchange_sum(exchange_sum(total, 1), 2), 4)
    shares, repeated = share_table(same_ids, combine_weights, total)
    received, repeated, shares = tied(received, repeated, shares)
    rows = opened(received)
    rows, repeated = tied(rows, repeated)
    half = between_chips(repeated).reshape(-1, WIDTH)
    hidden, first = experts(rows, gathered)
    hidden, first, half = tied(hidden, first, half)
    first = exchanged(first)
    second = exchanged(results(hidden, second_gathered))
    first_mix = mixed(shares, first)
    layer_out = mixed(shares, second, first_mix, latents)
    query_grad = both_halves(half)
    return (layer_out, query_grad)


def solution(mesh):
    return jax.shard_map(
        per_device,
        mesh=mesh,
        in_specs=(
            P(),
            P(("dp", "expert"), None),
            P(("dp", "expert"), None),
            P(),
            P("expert", "dp", None),
            P("expert", "dp", None),
            P("expert", None, "dp"),
            P(("dp", "expert"), None),
            P(("dp", "expert"), None),
            P(("dp", "expert"), None),
        ),
        out_specs=(P(("dp", "expert"), None), P()),
        check_vma=False,
    )
```

```python
import functools
import math

import jax
import jax.numpy as jnp
from jax import lax
from jax.experimental import pallas as pl
from jax.experimental.pallas import tpu as pltpu
from jax.sharding import PartitionSpec as P

HEADS = 20
HEAD_DIM = 128
WIDTH = HEADS * HEAD_DIM
ROWS = 128
PATCHES = 512
TOP = 6
EXPERTS = 32
HID = 832
CAPACITY = 28
N_DP = 8
SHARD = WIDTH // N_DP
HALVES = 2
BLOCK = HALVES * CAPACITY
GROUP = 8
GROUPS = EXPERTS // GROUP
GROUP_ROWS = GROUP * BLOCK
SMALL = 4
SMALL_ROWS = SMALL * BLOCK
SMALL_SLOTS = SMALL * CAPACITY
SLOTS = EXPERTS * CAPACITY
CHUNK = WIDTH // 2
SPLIT = (128, SHARD - 128)
MAIN = 768
REST = HID - MAIN
FIRST_MAIN = 2 * SHARD + SPLIT[0]
FIRST_REST = 64
FIRST_ROWS = FIRST_MAIN + FIRST_REST
SECOND_REST = 16
SECOND_ROWS = SPLIT[1] + SECOND_REST
EPSILON = 1e-06
SCALE = 1.0 / math.sqrt(HEAD_DIM)
HEADS_PER_STEP = 4
VMEM_LIMIT = 56 * 1024 * 1024

F32 = jnp.float32
BF16 = jnp.bfloat16


def dot(a, b):
    return jnp.dot(a, b, preferred_element_type=F32)


def dot_t(a, b):
    return lax.dot_general(a, b, (((1,), (1,)), ((), ())), preferred_element_type=F32)


def iota(shape, axis):
    return lax.broadcasted_iota(jnp.int32, shape, axis)


def over_28(value):
    return (value * 1171) >> 15


def over_56(value):
    return (value * 1171) >> 16


def head_weights(queries, near_keys, far_keys):
    near = dot_t(queries, near_keys) * SCALE
    far = dot_t(queries, far_keys) * SCALE
    peak = jnp.maximum(
        jnp.max(near, axis=1, keepdims=True), jnp.max(far, axis=1, keepdims=True)
    )
    near = jnp.exp(near - peak)
    far = jnp.exp(far - peak)
    total = jnp.sum(near, axis=1, keepdims=True) + jnp.sum(far, axis=1, keepdims=True)
    inverse = 1.0 / total
    return near * inverse, far * inverse


def attention_kernel(
    parity, queries, near_keys, far_keys, near_values, far_values, cotangent, latents, grad
):
    for head in range(HEADS_PER_STEP):
        at = slice(head * HEAD_DIM, (head + 1) * HEAD_DIM)
        near, far = head_weights(queries[:, at], near_keys[:, at], far_keys[:, at])
        attended = dot(near.astype(BF16), near_values[:, at]) + dot(
            far.astype(BF16), far_values[:, at]
        )
        rounded = attended.astype(BF16)
        latents[:, at] = rounded
        given = cotangent[:, at]
        inner = jnp.sum(given.astype(F32) * rounded.astype(F32), axis=1, keepdims=True)
        near = near * (dot_t(given, near_values[:, at]) - inner) * SCALE
        far = far * (dot_t(given, far_values[:, at]) - inner) * SCALE
        part = dot(near.astype(BF16), near_keys[:, at]) + dot(far.astype(BF16), far_keys[:, at])
        grad[:, at] = part.astype(BF16)


def attention(parity, queries, keys, far_keys, values, far_values, cotangent):
    wide = HEADS_PER_STEP * HEAD_DIM
    own = pl.BlockSpec((ROWS, wide), lambda i, parity: (0, i))
    patches = pl.BlockSpec((PATCHES, wide), lambda i, parity: (0, i))
    asked = pl.BlockSpec((ROWS, wide), lambda i, parity: (parity[0], i))
    return pl.pallas_call(
        attention_kernel,
        out_shape=(
            jax.ShapeDtypeStruct((ROWS, WIDTH), BF16),
            jax.ShapeDtypeStruct((ROWS, WIDTH), BF16),
        ),
        grid_spec=pltpu.PrefetchScalarGridSpec(
            num_scalar_prefetch=1,
            grid=(HEADS // HEADS_PER_STEP,),
            in_specs=[asked, patches, patches, patches, patches, own],
            out_specs=(own, own),
        ),
        compiler_params=pltpu.CompilerParams(vmem_limit_bytes=VMEM_LIMIT),
        cost_estimate=pl.CostEstimate(
            flops=2_684_354_560, bytes_accessed=13_000_000, transcendentals=2_621_440
        ),
    )(parity, queries, keys, far_keys, values, far_values, cotangent)


def slot_table(ids):
    named = jnp.zeros((ROWS, EXPERTS), F32)
    for choice in range(TOP):
        named = named + (ids[:, choice : choice + 1] == iota((ROWS, EXPERTS), 1)).astype(F32)
    earlier = (iota((ROWS, ROWS), 0) > iota((ROWS, ROWS), 1)).astype(BF16)
    before = dot(earlier, named.astype(BF16))
    return jnp.where(named > 0, before, -1.0)


def dispatch_kernel(latents, gain, ids, out, stacked, slots):
    at_group = pl.program_id(0)

    @pl.when(at_group == 0)
    def _():
        wide = latents[...].astype(F32)
        factor = lax.rsqrt(jnp.mean(wide * wide, axis=1, keepdims=True) + EPSILON)
        normed = (wide * factor * gain[...]).astype(BF16)
        stacked[:ROWS, :] = normed[:, :CHUNK]
        stacked[ROWS:, :] = normed[:, CHUNK:]
        slots[...] = slot_table(ids).astype(BF16)

    row = iota((GROUP_ROWS, 1), 0)
    expert_of = over_56(row)
    slot_of = row - over_28(row) * CAPACITY
    half_of = over_28(row) - expert_of * HALVES
    pick = (iota((GROUP_ROWS, EXPERTS), 1) == expert_of + at_group * GROUP).astype(BF16)
    match = dot_t(pick, slots[...]) == slot_of.astype(F32)
    chosen = jnp.concatenate(
        [jnp.where(match & (half_of == half), 1.0, 0.0) for half in range(HALVES)], axis=1
    )
    out[...] = dot(chosen.astype(BF16), stacked[...]).astype(BF16)


def dispatch(latents, gain, ids):
    return pl.pallas_call(
        dispatch_kernel,
        grid=(GROUPS,),
        in_specs=[
            pl.BlockSpec((ROWS, WIDTH), lambda i: (0, 0)),
            pl.BlockSpec((1, WIDTH), lambda i: (0, 0)),
            pl.BlockSpec((ROWS, TOP), lambda i: (0, 0)),
        ],
        out_specs=pl.BlockSpec((GROUP_ROWS, CHUNK), lambda i: (i, 0)),
        out_shape=jax.ShapeDtypeStruct((EXPERTS * BLOCK, CHUNK), BF16),
        scratch_shapes=[
            pltpu.VMEM((HALVES * ROWS, CHUNK), BF16),
            pltpu.VMEM((ROWS, EXPERTS), BF16),
        ],
        compiler_params=pltpu.CompilerParams(vmem_limit_bytes=VMEM_LIMIT),
        cost_estimate=pl.CostEstimate(
            flops=1_200_000_000, bytes_accessed=6_000_000, transcendentals=0
        ),
    )(latents, gain, ids)


HALF = SLOTS // 2


def whole_block(shape):
    return pl.BlockSpec(shape, lambda i: (0, 0))


def open_kernel(blocks, rows):
    for part in range(GROUP // SMALL):
        at, to = part * SMALL_ROWS, part * SMALL_SLOTS
        taken = blocks[at : at + SMALL_ROWS, :].astype(F32)
        for half in range(HALVES):
            pieces = [
                taken[block * BLOCK + half * CAPACITY : block * BLOCK + (half + 1) * CAPACITY, :]
                for block in range(SMALL)
            ]
            rows[to : to + SMALL_SLOTS, half * CHUNK : (half + 1) * CHUNK] = jnp.concatenate(
                pieces, axis=0
            ).astype(BF16)


def opened(received):
    return pl.pallas_call(
        open_kernel,
        grid=(GROUPS,),
        in_specs=[pl.BlockSpec((GROUP_ROWS, CHUNK), lambda i: (i, 0))],
        out_specs=pl.BlockSpec((GROUP_ROWS // HALVES, WIDTH), lambda i: (i, 0)),
        out_shape=jax.ShapeDtypeStruct((SLOTS, WIDTH), BF16),
        compiler_params=pltpu.CompilerParams(vmem_limit_bytes=VMEM_LIMIT),
        cost_estimate=pl.CostEstimate(
            flops=1_000_000_000, bytes_accessed=9_000_000, transcendentals=0
        ),
    )(received)


def close_rows(rows, out):
    width = rows.shape[1] // 2
    for pair in range(HALF // CAPACITY // 2):
        pieces = []
        for block in (2 * pair, 2 * pair + 1):
            taken = rows[block * CAPACITY : (block + 1) * CAPACITY, :]
            pieces += [taken[:, :width], taken[:, width:]]
        at = 2 * pair * BLOCK
        out[at : at + 2 * BLOCK, :] = jnp.concatenate(pieces, axis=0).astype(BF16)


def side_by_side(left, right):
    return jnp.concatenate([left.astype(F32), right.astype(F32)], axis=1).astype(BF16)


def right_side(block):
    return pltpu.roll(block.astype(F32), REST, 1)[:, :REST].astype(BF16)


def pack_kernel(
    gate, up, down, first, second, gates, ups, downs, first_rest, second_rest, sems, out_sems
):
    loads = [
        pltpu.make_async_copy(source, target, sems.at[index])
        for index, (source, target) in enumerate(((gate, gates), (up, ups), (down, downs)))
    ]
    for load in loads:
        load.start()
    outs = []

    def send(source, target):
        outs.append(pltpu.make_async_copy(source, target, out_sems.at[len(outs)]))
        outs[-1].start()

    main = pl.ds(0, MAIN)
    loads[0].wait()
    send(gates.at[:, main], first.at[pl.ds(0, SHARD), :])
    loads[1].wait()
    send(ups.at[:, main], first.at[pl.ds(SHARD, SHARD), :])
    loads[2].wait()
    send(downs.at[pl.ds(0, SPLIT[0]), main], first.at[pl.ds(2 * SHARD, SPLIT[0]), :])
    send(downs.at[pl.ds(SPLIT[0], SPLIT[1]), main], second.at[pl.ds(0, SPLIT[1]), :])
    rest = side_by_side(gates[:, MAIN:], ups[:, MAIN:])
    for block in range(SHARD // FIRST_REST):
        first_rest[:, block * 128 : (block + 1) * 128] = rest[
            block * FIRST_REST : (block + 1) * FIRST_REST, :
        ]
    first_rest[:, MAIN - 128 :] = side_by_side(
        downs[:FIRST_REST, MAIN:], downs[FIRST_REST : SPLIT[0], MAIN:]
    )
    send(first_rest, first.at[pl.ds(FIRST_MAIN, FIRST_REST), :])
    middle = SPLIT[0] + SPLIT[1] // 2
    rest = side_by_side(downs[SPLIT[0] : middle, MAIN:], downs[middle:, MAIN:])
    for block in range(MAIN // 128):
        second_rest[:, block * 128 : (block + 1) * 128] = rest[
            block * SECOND_REST : (block + 1) * SECOND_REST, :
        ]
    send(second_rest, second.at[pl.ds(SPLIT[1], SECOND_REST), :])
    for out in outs:
        out.wait()


def packed(gate, up, down):
    hbm = pl.BlockSpec(memory_space=pltpu.HBM)
    return pl.pallas_call(
        pack_kernel,
        out_shape=(
            jax.ShapeDtypeStruct((FIRST_ROWS, MAIN), BF16),
            jax.ShapeDtypeStruct((SECOND_ROWS, MAIN), BF16),
        ),
        in_specs=[hbm] * 3,
        out_specs=(hbm, hbm),
        scratch_shapes=[pltpu.VMEM((SHARD, HID), BF16)] * 3
        + [
            pltpu.VMEM((FIRST_REST, MAIN), BF16),
            pltpu.VMEM((SECOND_REST, MAIN), BF16),
            pltpu.SemaphoreType.DMA((3,)),
            pltpu.SemaphoreType.DMA((6,)),
        ],
        compiler_params=pltpu.CompilerParams(vmem_limit_bytes=VMEM_LIMIT),
        cost_estimate=pl.CostEstimate(flops=0, bytes_accessed=3_200_000, transcendentals=0),
    )(gate, up, down)


def expert_kernel(
    rows, gathered, units, out,
    taken, full, rests, blocks, down, down_rest, gates, hidden, outs, sems, out_sems,
):
    row_copies = [
        pltpu.make_async_copy(
            rows.at[pl.ds(half * HALF, HALF), :],
            taken.at[pl.ds(half * HALF, HALF), :],
            sems.at[half],
        )
        for half in range(2)
    ]
    gate_copies, up_copies, rest_copies = [], [], []
    for shard in range(N_DP):
        start = shard * FIRST_ROWS
        for which, copies in enumerate((gate_copies, up_copies)):
            copies.append(
                pltpu.make_async_copy(
                    gathered.at[pl.ds(start + which * SHARD, SHARD), :],
                    full.at[which, pl.ds(shard * SHARD, SHARD), :],
                    sems.at[2 + 4 * shard + which],
                )
            )
        rest_copies.append(
            pltpu.make_async_copy(
                gathered.at[pl.ds(start + FIRST_MAIN, FIRST_REST), :],
                blocks.at[shard],
                sems.at[2 + 4 * shard + 2],
            )
        )
        rest_copies.append(
            pltpu.make_async_copy(
                gathered.at[pl.ds(start + 2 * SHARD, SPLIT[0]), :],
                down.at[pl.ds(shard * SPLIT[0], SPLIT[0]), :],
                sems.at[2 + 4 * shard + 3],
            )
        )
    for copy in [row_copies[0]] + gate_copies + [row_copies[1]] + up_copies + rest_copies:
        copy.start()
    for copy in [row_copies[0]] + gate_copies:
        copy.wait()
    gates[:HALF, :] = dot(taken[:HALF, :], full[0])
    row_copies[1].wait()
    gates[HALF:, :] = dot(taken[HALF:, :], full[0])
    for copy in up_copies + rest_copies:
        copy.wait()
    for shard in range(N_DP):
        for block in range(SHARD // FIRST_REST):
            at = shard * SHARD + block * FIRST_REST
            rests[at : at + FIRST_REST, :] = blocks[shard, :, block * 128 : (block + 1) * 128]
        last = blocks[shard, :, MAIN - 128 :]
        at = shard * SPLIT[0]
        down_rest[at : at + FIRST_REST, :] = last[:, :REST]
        down_rest[at + FIRST_REST : at + SPLIT[0], :] = right_side(last)
    gate = gates[...]
    up = dot(taken[...], full[1])
    hidden[:, :MAIN] = (gate * (0.5 + 0.5 * jnp.tanh(0.5 * gate)) * up).astype(BF16)
    both = dot(taken[...], rests[...])
    gate, up = both[:, :REST], pltpu.roll(both, REST, 1)[:, :REST]
    hidden[:, MAIN:] = (gate * (0.5 + 0.5 * jnp.tanh(0.5 * gate)) * up).astype(BF16)
    out_copies = [pltpu.make_async_copy(hidden, units, out_sems.at[2])]
    out_copies[0].start()
    for half in range(2):
        at = slice(half * HALF, (half + 1) * HALF)
        result = dot_t(hidden[at, :MAIN], down[...]) + dot_t(hidden[at, MAIN:], down_rest[...])
        close_rows(result, outs.at[half])
        copy = pltpu.make_async_copy(
            outs.at[half],
            out.at[pl.ds(half * HALF * HALVES, HALF * HALVES), :],
            out_sems.at[half],
        )
        copy.start()
        out_copies.append(copy)
    for copy in out_copies:
        copy.wait()


def experts(rows, gathered):
    columns = N_DP * SPLIT[0]
    hbm = pl.BlockSpec(memory_space=pltpu.HBM)
    return pl.pallas_call(
        expert_kernel,
        out_shape=(
            jax.ShapeDtypeStruct((SLOTS, HID), BF16),
            jax.ShapeDtypeStruct((EXPERTS * BLOCK, columns // 2), BF16),
        ),
        in_specs=[hbm, hbm],
        out_specs=(hbm, hbm),
        scratch_shapes=[
            pltpu.VMEM((SLOTS, WIDTH), BF16),
            pltpu.VMEM((2, WIDTH, MAIN), BF16),
            pltpu.VMEM((WIDTH, 2 * REST), BF16),
            pltpu.VMEM((N_DP, FIRST_REST, MAIN), BF16),
            pltpu.VMEM((columns, MAIN), BF16),
            pltpu.VMEM((columns, REST), BF16),
            pltpu.VMEM((SLOTS, MAIN), F32),
            pltpu.VMEM((SLOTS, HID), BF16),
            pltpu.VMEM((2, HALF * HALVES, columns // 2), BF16),
            pltpu.SemaphoreType.DMA((2 + 4 * N_DP,)),
            pltpu.SemaphoreType.DMA((3,)),
        ],
        compiler_params=pltpu.CompilerParams(vmem_limit_bytes=VMEM_LIMIT),
        cost_estimate=pl.CostEstimate(
            flops=10_000_000_000, bytes_accessed=20_000_000, transcendentals=745_472
        ),
    )(rows, gathered)


def result_kernel(hidden, gathered, out, units, full, rest, blocks, outs, sems, out_sems):
    unit_copies = [
        pltpu.make_async_copy(
            hidden.at[pl.ds(half * HALF, HALF), :],
            units.at[pl.ds(half * HALF, HALF), :],
            sems.at[2 * N_DP + half],
        )
        for half in range(2)
    ]
    copies, rest_copies = [], []
    for shard in range(N_DP):
        start = shard * SECOND_ROWS
        copies.append(
            pltpu.make_async_copy(
                gathered.at[pl.ds(start, SPLIT[1]), :],
                full.at[pl.ds(shard * SPLIT[1], SPLIT[1]), :],
                sems.at[2 * shard],
            )
        )
        rest_copies.append(
            pltpu.make_async_copy(
                gathered.at[pl.ds(start + SPLIT[1], SECOND_REST), :],
                blocks.at[shard],
                sems.at[2 * shard + 1],
            )
        )
    for copy in rest_copies + [unit_copies[0]] + copies + [unit_copies[1]]:
        copy.start()
    for copy in rest_copies:
        copy.wait()
    for shard in range(N_DP):
        for block in range(MAIN // 128):
            at = shard * SPLIT[1] + block * SECOND_REST
            middle = at + SPLIT[1] // 2
            both = blocks[shard, :, block * 128 : (block + 1) * 128]
            rest[at : at + SECOND_REST, :] = both[:, :REST]
            rest[middle : middle + SECOND_REST, :] = right_side(both)
    for copy in [unit_copies[0]] + copies:
        copy.wait()
    out_copies = []
    for half in range(2):
        if half == 1:
            unit_copies[1].wait()
        at = slice(half * HALF, (half + 1) * HALF)
        result = dot_t(units[at, :MAIN], full[...]) + dot_t(units[at, MAIN:], rest[...])
        close_rows(result, outs.at[half])
        copy = pltpu.make_async_copy(
            outs.at[half],
            out.at[pl.ds(half * HALF * HALVES, HALF * HALVES), :],
            out_sems.at[half],
        )
        copy.start()
        out_copies.append(copy)
    for copy in out_copies:
        copy.wait()


def results(hidden, gathered):
    columns = N_DP * SPLIT[1]
    hbm = pl.BlockSpec(memory_space=pltpu.HBM)
    return pl.pallas_call(
        result_kernel,
        out_shape=jax.ShapeDtypeStruct((EXPERTS * BLOCK, columns // 2), BF16),
        in_specs=[hbm, hbm],
        out_specs=hbm,
        scratch_shapes=[
            pltpu.VMEM((SLOTS, HID), BF16),
            pltpu.VMEM((columns, MAIN), BF16),
            pltpu.VMEM((columns, REST), BF16),
            pltpu.VMEM((N_DP, SECOND_REST, MAIN), BF16),
            pltpu.VMEM((2, HALF * HALVES, columns // 2), BF16),
            pltpu.SemaphoreType.DMA((2 * N_DP + 2,)),
            pltpu.SemaphoreType.DMA((2,)),
        ],
        compiler_params=pltpu.CompilerParams(vmem_limit_bytes=63 * 1024 * 1024),
        cost_estimate=pl.CostEstimate(
            flops=3_000_000_000, bytes_accessed=8_000_000, transcendentals=0
        ),
    )(hidden, gathered)


TERMS = 2
SHARE_ROWS = TERMS * ROWS


def share_kernel(ids, weights, total, out, repeated, slots, terms):
    at_group = pl.program_id(0)
    for copy in range(EXPERTS // 2 // GROUPS):
        repeated[copy] = total[...].astype(BF16)

    @pl.when(at_group == 0)
    def _():
        slots[...] = slot_table(ids).astype(BF16)
        shares = jnp.zeros((ROWS, EXPERTS), F32)
        for choice in range(TOP):
            named = ids[:, choice : choice + 1] == iota((ROWS, EXPERTS), 1)
            shares = shares + jnp.where(named, weights[:, choice : choice + 1], 0.0)
        high = shares.astype(BF16)
        terms[:ROWS, :] = high
        terms[ROWS:, :] = (shares - high.astype(F32)).astype(BF16)

    row = iota((EXPERTS, GROUP_ROWS), 1)
    pick = (over_56(row) + at_group * GROUP == iota((EXPERTS, GROUP_ROWS), 0)).astype(BF16)
    lane = iota((ROWS, GROUP_ROWS), 1)
    slot_of = lane - over_28(lane) * CAPACITY
    match = dot(slots[...], pick) == slot_of.astype(F32)
    shares = dot(terms[...], pick)
    for term in range(TERMS):
        at = slice(term * ROWS, (term + 1) * ROWS)
        out[at, :] = jnp.where(match, shares[at], 0.0).astype(BF16)


def share_table(ids, weights, total):
    chips = EXPERTS // 2
    return pl.pallas_call(
        share_kernel,
        grid=(GROUPS,),
        in_specs=[
            whole_block((ROWS, TOP)),
            whole_block((ROWS, TOP)),
            whole_block(total.shape),
        ],
        out_specs=(
            pl.BlockSpec((SHARE_ROWS, GROUP_ROWS), lambda i: (i, 0)),
            pl.BlockSpec((chips // GROUPS,) + total.shape, lambda i: (i, 0, 0)),
        ),
        out_shape=(
            jax.ShapeDtypeStruct((GROUPS * SHARE_ROWS, GROUP_ROWS), BF16),
            jax.ShapeDtypeStruct((chips,) + total.shape, BF16),
        ),
        scratch_shapes=[
            pltpu.VMEM((ROWS, EXPERTS), BF16),
            pltpu.VMEM((TERMS * ROWS, EXPERTS), BF16),
        ],
        compiler_params=pltpu.CompilerParams(vmem_limit_bytes=VMEM_LIMIT),
        cost_estimate=pl.CostEstimate(
            flops=50_000_000, bytes_accessed=3_000_000, transcendentals=0
        ),
    )(ids, weights, total)


def mix_blocks(shares, returned, table, blocks, total, sems, later=()):
    share_copies = [
        pltpu.make_async_copy(
            shares.at[pl.ds(g * SHARE_ROWS, SHARE_ROWS), :],
            table.at[pl.ds(g * SHARE_ROWS, SHARE_ROWS), :],
            sems.at[g],
        )
        for g in range(GROUPS)
    ]
    copies = [
        pltpu.make_async_copy(
            returned.at[pl.ds(g * GROUP_ROWS, GROUP_ROWS), :],
            blocks.at[pl.ds(g * GROUP_ROWS, GROUP_ROWS), :],
            sems.at[GROUPS + g],
        )
        for g in range(GROUPS)
    ]
    for g in range(GROUPS):
        share_copies[g].start()
        copies[g].start()
    for copy in later:
        copy.start()
    row = iota((1, GROUP_ROWS), 1)
    half_of = over_28(row) - over_56(row) * HALVES
    masks = [(half_of == half).astype(BF16) for half in range(HALVES)]
    for g in range(GROUPS):
        share_copies[g].wait()
        copies[g].wait()
        counts = table[g * SHARE_ROWS : (g + 1) * SHARE_ROWS, :]
        counts = jnp.concatenate([counts * mask for mask in masks], axis=0)
        found = dot(counts, blocks[g * GROUP_ROWS : (g + 1) * GROUP_ROWS, :])
        for half in range(HALVES):
            at = half * SHARE_ROWS
            part = found[at : at + ROWS] + found[at + ROWS : at + SHARE_ROWS]
            at = slice(half * ROWS, (half + 1) * ROWS)
            total[at, :] = part if g == 0 else total[at, :] + part
    for copy in later:
        copy.wait()


def mix_kernel(shares, returned, out, table, blocks, total, sems):
    mix_blocks(shares, returned, table, blocks, total, sems)
    width = returned.shape[1]
    out[:, :width] = total[:ROWS, :]
    out[:, width:] = total[ROWS:, :]


def last_kernel(
    shares, returned, first, latents, out, table, blocks, total, sems, others, own, last_sems
):
    copies = [
        pltpu.make_async_copy(first, others, last_sems.at[0]),
        pltpu.make_async_copy(latents, own, last_sems.at[1]),
    ]
    mix_blocks(shares, returned, table, blocks, total, sems, copies)
    pieces = []
    for shard in range(N_DP):
        half, at = shard // 4, shard % 4 * SPLIT[1]
        pieces.append(others[:, shard * SPLIT[0] : (shard + 1) * SPLIT[0]])
        pieces.append(total[half * ROWS : (half + 1) * ROWS, at : at + SPLIT[1]])
    whole = jnp.concatenate(pieces, axis=1)
    out[...] = (own[...].astype(F32) + whole).astype(BF16)


def mixed(shares, returned, *last):
    width = returned.shape[1]
    hbm = pl.BlockSpec(memory_space=pltpu.HBM)
    out, kernel = jax.ShapeDtypeStruct((ROWS, 2 * width), F32), mix_kernel
    scratch = [
        pltpu.VMEM(shares.shape, BF16),
        pltpu.VMEM(returned.shape, BF16),
        pltpu.VMEM((HALVES * ROWS, width), F32),
        pltpu.SemaphoreType.DMA((2 * GROUPS,)),
    ]
    if last:
        out, kernel = jax.ShapeDtypeStruct((ROWS, WIDTH), BF16), last_kernel
        scratch += [pltpu.VMEM(value.shape, value.dtype) for value in last]
        scratch += [pltpu.SemaphoreType.DMA((2,))]
    return pl.pallas_call(
        kernel,
        in_specs=[hbm] * (2 + len(last)),
        out_shape=out,
        out_specs=pl.BlockSpec(memory_space=pltpu.VMEM),
        scratch_shapes=scratch,
        compiler_params=pltpu.CompilerParams(vmem_limit_bytes=63 * 1024 * 1024),
        cost_estimate=pl.CostEstimate(
            flops=1_200_000_000, bytes_accessed=4_000_000, transcendentals=0
        ),
    )(shares, returned, *last)


SAME_CORE = [list(range(core, EXPERTS, 2)) for core in range(2)]


def other_core(value):
    return lax.ppermute(value, "expert", [(at, at ^ 1) for at in range(EXPERTS)])


def between_chips(pieces):
    return lax.all_to_all(
        pieces,
        "expert",
        split_axis=0,
        concat_axis=0,
        tiled=True,
        axis_index_groups=SAME_CORE,
    )


def scattered(part):
    pieces = between_chips(part.reshape(EXPERTS // 2, -1, WIDTH))
    return jnp.sum(pieces.astype(F32), axis=0)


def exchange_sum(total, bit):
    return total + lax.ppermute(total, "dp", [(at, at ^ bit) for at in range(N_DP)])


def both_halves(half):
    far_half = other_core(half)
    low = lax.axis_index("expert") % 2 == 0
    whole = jnp.concatenate(
        [jnp.where(low, half, far_half), jnp.where(low, far_half, half)], axis=0
    )
    return whole.astype(F32)


def exchanged(blocks):
    rows, columns = blocks.shape
    return lax.all_to_all(
        blocks.reshape(EXPERTS, rows // EXPERTS, columns),
        "expert",
        split_axis=0,
        concat_axis=0,
        tiled=True,
    ).reshape(rows, columns)


def tied(*values):
    return lax.optimization_barrier(values)


def per_device(
    queries,
    patch_keys,
    patch_values,
    norm_gain,
    gate_weight,
    up_weight,
    down_weight,
    expert_ids,
    combine_weights,
    latent_grad,
):
    parity = lax.axis_index("expert") % 2
    which = parity.reshape(1).astype(jnp.int32)
    far_keys, far_values = other_core(patch_keys), other_core(patch_values)
    shard, second_shard = packed(gate_weight[0], up_weight[0], down_weight[0].T)
    gathered = lax.all_gather(shard, "dp", axis=0, tiled=True)
    patches = (which, queries, patch_keys, far_keys, patch_values, far_values)
    latents, grad_part = attention(*patches, latent_grad)
    latents, second_shard = tied(latents, second_shard)
    second_gathered = lax.all_gather(second_shard, "dp", axis=0, tiled=True)
    total = scattered(grad_part)
    sent = dispatch(latents, norm_gain.reshape(1, WIDTH), expert_ids)
    sent, total, same_ids = tied(sent, total, expert_ids)
    received = exchanged(sent)
    total = exchange_sum(exchange_sum(exchange_sum(total, 1), 2), 4)
    shares, repeated = share_table(same_ids, combine_weights, total)
    received, repeated, shares = tied(received, repeated, shares)
    rows = opened(received)
    rows, repeated = tied(rows, repeated)
    half = between_chips(repeated).reshape(-1, WIDTH)
    hidden, first = experts(rows, gathered)
    hidden, first, half = tied(hidden, first, half)
    first = exchanged(first)
    second = exchanged(results(hidden, second_gathered))
    first_mix = mixed(shares, first)
    layer_out = mixed(shares, second, first_mix, latents)
    query_grad = both_halves(half)
    return (layer_out, query_grad)


def solution(mesh):
    return jax.shard_map(
        per_device,
        mesh=mesh,
        in_specs=(
            P(),
            P(("dp", "expert"), None),
            P(("dp", "expert"), None),
            P(),
            P("expert", "dp", None),
            P("expert", "dp", None),
            P("expert", None, "dp"),
            P(("dp", "expert"), None),
            P(("dp", "expert"), None),
            P(("dp", "expert"), None),
        ),
        out_specs=(P(("dp", "expert"), None), P()),
        check_vma=False,
    )
```

```python
import functools
import math

import jax
import jax.numpy as jnp
from jax import lax
from jax.experimental import pallas as pl
from jax.experimental.pallas import tpu as pltpu
from jax.sharding import PartitionSpec as P

HEADS = 20
HEAD_DIM = 128
WIDTH = HEADS * HEAD_DIM
ROWS = 128
PATCHES = 512
TOP = 6
EXPERTS = 32
HID = 832
CAPACITY = 28
N_DP = 8
SHARD = WIDTH // N_DP
HALVES = 2
BLOCK = HALVES * CAPACITY
GROUP = 8
GROUPS = EXPERTS // GROUP
GROUP_ROWS = GROUP * BLOCK
SMALL = 4
SMALL_ROWS = SMALL * BLOCK
SMALL_SLOTS = SMALL * CAPACITY
SLOTS = EXPERTS * CAPACITY
CHUNK = WIDTH // 2
SPLIT = (128, SHARD - 128)
MAIN = 768
REST = HID - MAIN
FIRST_MAIN = 2 * SHARD + SPLIT[0]
FIRST_REST = 64
FIRST_ROWS = FIRST_MAIN + FIRST_REST
SECOND_REST = 16
SECOND_ROWS = SPLIT[1] + SECOND_REST
EPSILON = 1e-06
SCALE = 1.0 / math.sqrt(HEAD_DIM)
HEADS_PER_STEP = 4
VMEM_LIMIT = 56 * 1024 * 1024

F32 = jnp.float32
BF16 = jnp.bfloat16


def dot(a, b):
    return jnp.dot(a, b, preferred_element_type=F32)


def dot_t(a, b):
    return lax.dot_general(a, b, (((1,), (1,)), ((), ())), preferred_element_type=F32)


def iota(shape, axis):
    return lax.broadcasted_iota(jnp.int32, shape, axis)


def over_28(value):
    return (value * 1171) >> 15


def over_56(value):
    return (value * 1171) >> 16


def head_weights(queries, near_keys, far_keys):
    near = dot_t(queries, near_keys) * SCALE
    far = dot_t(queries, far_keys) * SCALE
    peak = jnp.maximum(
        jnp.max(near, axis=1, keepdims=True), jnp.max(far, axis=1, keepdims=True)
    )
    near = jnp.exp(near - peak)
    far = jnp.exp(far - peak)
    total = jnp.sum(near, axis=1, keepdims=True) + jnp.sum(far, axis=1, keepdims=True)
    inverse = 1.0 / total
    return near * inverse, far * inverse


def attention_kernel(
    parity, queries, near_keys, far_keys, near_values, far_values, cotangent, latents, grad
):
    for head in range(HEADS_PER_STEP):
        at = slice(head * HEAD_DIM, (head + 1) * HEAD_DIM)
        near, far = head_weights(queries[:, at], near_keys[:, at], far_keys[:, at])
        attended = dot(near.astype(BF16), near_values[:, at]) + dot(
            far.astype(BF16), far_values[:, at]
        )
        rounded = attended.astype(BF16)
        latents[:, at] = rounded
        given = cotangent[:, at]
        inner = jnp.sum(given.astype(F32) * rounded.astype(F32), axis=1, keepdims=True)
        near = near * (dot_t(given, near_values[:, at]) - inner) * SCALE
        far = far * (dot_t(given, far_values[:, at]) - inner) * SCALE
        part = dot(near.astype(BF16), near_keys[:, at]) + dot(far.astype(BF16), far_keys[:, at])
        grad[:, at] = part.astype(BF16)


def attention(parity, queries, keys, far_keys, values, far_values, cotangent):
    wide = HEADS_PER_STEP * HEAD_DIM
    own = pl.BlockSpec((ROWS, wide), lambda i, parity: (0, i))
    patches = pl.BlockSpec((PATCHES, wide), lambda i, parity: (0, i))
    asked = pl.BlockSpec((ROWS, wide), lambda i, parity: (parity[0], i))
    return pl.pallas_call(
        attention_kernel,
        out_shape=(
            jax.ShapeDtypeStruct((ROWS, WIDTH), BF16),
            jax.ShapeDtypeStruct((ROWS, WIDTH), BF16),
        ),
        grid_spec=pltpu.PrefetchScalarGridSpec(
            num_scalar_prefetch=1,
            grid=(HEADS // HEADS_PER_STEP,),
            in_specs=[asked, patches, patches, patches, patches, own],
            out_specs=(own, own),
        ),
        compiler_params=pltpu.CompilerParams(vmem_limit_bytes=VMEM_LIMIT),
        cost_estimate=pl.CostEstimate(
            flops=2_684_354_560, bytes_accessed=13_000_000, transcendentals=2_621_440
        ),
    )(parity, queries, keys, far_keys, values, far_values, cotangent)


def slot_table(ids):
    named = jnp.zeros((ROWS, EXPERTS), F32)
    for choice in range(TOP):
        named = named + (ids[:, choice : choice + 1] == iota((ROWS, EXPERTS), 1)).astype(F32)
    earlier = (iota((ROWS, ROWS), 0) > iota((ROWS, ROWS), 1)).astype(BF16)
    before = dot(earlier, named.astype(BF16))
    return jnp.where(named > 0, before, -1.0)


def dispatch_kernel(latents, gain, ids, out, stacked, slots):
    at_group = pl.program_id(0)

    @pl.when(at_group == 0)
    def _():
        wide = latents[...].astype(F32)
        factor = lax.rsqrt(jnp.mean(wide * wide, axis=1, keepdims=True) + EPSILON)
        normed = (wide * factor * gain[...]).astype(BF16)
        stacked[:ROWS, :] = normed[:, :CHUNK]
        stacked[ROWS:, :] = normed[:, CHUNK:]
        slots[...] = slot_table(ids).astype(BF16)

    row = iota((GROUP_ROWS, 1), 0)
    expert_of = over_56(row)
    slot_of = row - over_28(row) * CAPACITY
    half_of = over_28(row) - expert_of * HALVES
    pick = (iota((GROUP_ROWS, EXPERTS), 1) == expert_of + at_group * GROUP).astype(BF16)
    match = dot_t(pick, slots[...]) == slot_of.astype(F32)
    chosen = jnp.concatenate(
        [jnp.where(match & (half_of == half), 1.0, 0.0) for half in range(HALVES)], axis=1
    )
    out[...] = dot(chosen.astype(BF16), stacked[...]).astype(BF16)


def dispatch(latents, gain, ids):
    return pl.pallas_call(
        dispatch_kernel,
        grid=(GROUPS,),
        in_specs=[
            pl.BlockSpec((ROWS, WIDTH), lambda i: (0, 0)),
            pl.BlockSpec((1, WIDTH), lambda i: (0, 0)),
            pl.BlockSpec((ROWS, TOP), lambda i: (0, 0)),
        ],
        out_specs=pl.BlockSpec((GROUP_ROWS, CHUNK), lambda i: (i, 0)),
        out_shape=jax.ShapeDtypeStruct((EXPERTS * BLOCK, CHUNK), BF16),
        scratch_shapes=[
            pltpu.VMEM((HALVES * ROWS, CHUNK), BF16),
            pltpu.VMEM((ROWS, EXPERTS), BF16),
        ],
        compiler_params=pltpu.CompilerParams(vmem_limit_bytes=VMEM_LIMIT),
        cost_estimate=pl.CostEstimate(
            flops=1_200_000_000, bytes_accessed=6_000_000, transcendentals=0
        ),
    )(latents, gain, ids)


HALF = SLOTS // 2


def whole_block(shape):
    return pl.BlockSpec(shape, lambda i: (0, 0))


def open_kernel(blocks, rows):
    for part in range(GROUP // SMALL):
        at, to = part * SMALL_ROWS, part * SMALL_SLOTS
        taken = blocks[at : at + SMALL_ROWS, :].astype(F32)
        for half in range(HALVES):
            pieces = [
                taken[block * BLOCK + half * CAPACITY : block * BLOCK + (half + 1) * CAPACITY, :]
                for block in range(SMALL)
            ]
            rows[to : to + SMALL_SLOTS, half * CHUNK : (half + 1) * CHUNK] = jnp.concatenate(
                pieces, axis=0
            ).astype(BF16)


def opened(received):
    return pl.pallas_call(
        open_kernel,
        grid=(GROUPS,),
        in_specs=[pl.BlockSpec((GROUP_ROWS, CHUNK), lambda i: (i, 0))],
        out_specs=pl.BlockSpec((GROUP_ROWS // HALVES, WIDTH), lambda i: (i, 0)),
        out_shape=jax.ShapeDtypeStruct((SLOTS, WIDTH), BF16),
        compiler_params=pltpu.CompilerParams(vmem_limit_bytes=VMEM_LIMIT),
        cost_estimate=pl.CostEstimate(
            flops=1_000_000_000, bytes_accessed=9_000_000, transcendentals=0
        ),
    )(received)


def close_rows(rows, out):
    width = rows.shape[1] // 2
    for pair in range(HALF // CAPACITY // 2):
        pieces = []
        for block in (2 * pair, 2 * pair + 1):
            taken = rows[block * CAPACITY : (block + 1) * CAPACITY, :]
            pieces += [taken[:, :width], taken[:, width:]]
        at = 2 * pair * BLOCK
        out[at : at + 2 * BLOCK, :] = jnp.concatenate(pieces, axis=0).astype(BF16)


def side_by_side(left, right):
    return jnp.concatenate([left.astype(F32), right.astype(F32)], axis=1).astype(BF16)


def right_side(block):
    return pltpu.roll(block.astype(F32), REST, 1)[:, :REST].astype(BF16)


def pack_kernel(
    gate, up, down, first, second, gates, ups, downs, first_rest, second_rest, sems, out_sems
):
    loads = [
        pltpu.make_async_copy(source, target, sems.at[index])
        for index, (source, target) in enumerate(((gate, gates), (up, ups), (down, downs)))
    ]
    for load in loads:
        load.start()
    outs = []

    def send(source, target):
        outs.append(pltpu.make_async_copy(source, target, out_sems.at[len(outs)]))
        outs[-1].start()

    main = pl.ds(0, MAIN)
    loads[0].wait()
    send(gates.at[:, main], first.at[pl.ds(0, SHARD), :])
    loads[1].wait()
    send(ups.at[:, main], first.at[pl.ds(SHARD, SHARD), :])
    loads[2].wait()
    send(downs.at[pl.ds(0, SPLIT[0]), main], first.at[pl.ds(2 * SHARD, SPLIT[0]), :])
    send(downs.at[pl.ds(SPLIT[0], SPLIT[1]), main], second.at[pl.ds(0, SPLIT[1]), :])
    rest = side_by_side(gates[:, MAIN:], ups[:, MAIN:])
    for block in range(SHARD // FIRST_REST):
        first_rest[:, block * 128 : (block + 1) * 128] = rest[
            block * FIRST_REST : (block + 1) * FIRST_REST, :
        ]
    first_rest[:, MAIN - 128 :] = side_by_side(
        downs[:FIRST_REST, MAIN:], downs[FIRST_REST : SPLIT[0], MAIN:]
    )
    send(first_rest, first.at[pl.ds(FIRST_MAIN, FIRST_REST), :])
    middle = SPLIT[0] + SPLIT[1] // 2
    rest = side_by_side(downs[SPLIT[0] : middle, MAIN:], downs[middle:, MAIN:])
    for block in range(MAIN // 128):
        second_rest[:, block * 128 : (block + 1) * 128] = rest[
            block * SECOND_REST : (block + 1) * SECOND_REST, :
        ]
    send(second_rest, second.at[pl.ds(SPLIT[1], SECOND_REST), :])
    for out in outs:
        out.wait()


def packed(gate, up, down):
    hbm = pl.BlockSpec(memory_space=pltpu.HBM)
    return pl.pallas_call(
        pack_kernel,
        out_shape=(
            jax.ShapeDtypeStruct((FIRST_ROWS, MAIN), BF16),
            jax.ShapeDtypeStruct((SECOND_ROWS, MAIN), BF16),
        ),
        in_specs=[hbm] * 3,
        out_specs=(hbm, hbm),
        scratch_shapes=[pltpu.VMEM((SHARD, HID), BF16)] * 3
        + [
            pltpu.VMEM((FIRST_REST, MAIN), BF16),
            pltpu.VMEM((SECOND_REST, MAIN), BF16),
            pltpu.SemaphoreType.DMA((3,)),
            pltpu.SemaphoreType.DMA((6,)),
        ],
        compiler_params=pltpu.CompilerParams(vmem_limit_bytes=VMEM_LIMIT),
        cost_estimate=pl.CostEstimate(flops=0, bytes_accessed=3_200_000, transcendentals=0),
    )(gate, up, down)


def expert_kernel(
    rows, gathered, units, out,
    taken, full, rests, blocks, down, down_rest, gates, hidden, outs, sems, out_sems,
):
    row_copies = [
        pltpu.make_async_copy(
            rows.at[pl.ds(half * HALF, HALF), :],
            taken.at[pl.ds(half * HALF, HALF), :],
            sems.at[half],
        )
        for half in range(2)
    ]
    gate_copies, up_copies, rest_copies = [], [], []
    for shard in range(N_DP):
        start = shard * FIRST_ROWS
        for which, copies in enumerate((gate_copies, up_copies)):
            copies.append(
                pltpu.make_async_copy(
                    gathered.at[pl.ds(start + which * SHARD, SHARD), :],
                    full.at[which, pl.ds(shard * SHARD, SHARD), :],
                    sems.at[2 + 4 * shard + which],
                )
            )
        rest_copies.append(
            pltpu.make_async_copy(
                gathered.at[pl.ds(start + FIRST_MAIN, FIRST_REST), :],
                blocks.at[shard],
                sems.at[2 + 4 * shard + 2],
            )
        )
        rest_copies.append(
            pltpu.make_async_copy(
                gathered.at[pl.ds(start + 2 * SHARD, SPLIT[0]), :],
                down.at[pl.ds(shard * SPLIT[0], SPLIT[0]), :],
                sems.at[2 + 4 * shard + 3],
            )
        )
    for copy in [row_copies[0]] + gate_copies + [row_copies[1]] + up_copies + rest_copies:
        copy.start()
    for copy in [row_copies[0]] + gate_copies:
        copy.wait()
    gates[:HALF, :] = dot(taken[:HALF, :], full[0])
    row_copies[1].wait()
    gates[HALF:, :] = dot(taken[HALF:, :], full[0])
    for copy in up_copies + rest_copies:
        copy.wait()
    for shard in range(N_DP):
        for block in range(SHARD // FIRST_REST):
            at = shard * SHARD + block * FIRST_REST
            rests[at : at + FIRST_REST, :] = blocks[shard, :, block * 128 : (block + 1) * 128]
        last = blocks[shard, :, MAIN - 128 :]
        at = shard * SPLIT[0]
        down_rest[at : at + FIRST_REST, :] = last[:, :REST]
        down_rest[at + FIRST_REST : at + SPLIT[0], :] = right_side(last)
    gate = gates[...]
    up = dot(taken[...], full[1])
    hidden[:, :MAIN] = (gate * (0.5 + 0.5 * jnp.tanh(0.5 * gate)) * up).astype(BF16)
    both = dot(taken[...], rests[...])
    gate, up = both[:, :REST], pltpu.roll(both, REST, 1)[:, :REST]
    hidden[:, MAIN:] = (gate * (0.5 + 0.5 * jnp.tanh(0.5 * gate)) * up).astype(BF16)
    out_copies = [pltpu.make_async_copy(hidden, units, out_sems.at[2])]
    out_copies[0].start()
    for half in range(2):
        at = slice(half * HALF, (half + 1) * HALF)
        result = dot_t(hidden[at, :MAIN], down[...]) + dot_t(hidden[at, MAIN:], down_rest[...])
        close_rows(result, outs.at[half])
        copy = pltpu.make_async_copy(
            outs.at[half],
            out.at[pl.ds(half * HALF * HALVES, HALF * HALVES), :],
            out_sems.at[half],
        )
        copy.start()
        out_copies.append(copy)
    for copy in out_copies:
        copy.wait()


def experts(rows, gathered):
    columns = N_DP * SPLIT[0]
    hbm = pl.BlockSpec(memory_space=pltpu.HBM)
    return pl.pallas_call(
        expert_kernel,
        out_shape=(
            jax.ShapeDtypeStruct((SLOTS, HID), BF16),
            jax.ShapeDtypeStruct((EXPERTS * BLOCK, columns // 2), BF16),
        ),
        in_specs=[hbm, hbm],
        out_specs=(hbm, hbm),
        scratch_shapes=[
            pltpu.VMEM((SLOTS, WIDTH), BF16),
            pltpu.VMEM((2, WIDTH, MAIN), BF16),
            pltpu.VMEM((WIDTH, 2 * REST), BF16),
            pltpu.VMEM((N_DP, FIRST_REST, MAIN), BF16),
            pltpu.VMEM((columns, MAIN), BF16),
            pltpu.VMEM((columns, REST), BF16),
            pltpu.VMEM((SLOTS, MAIN), F32),
            pltpu.VMEM((SLOTS, HID), BF16),
            pltpu.VMEM((2, HALF * HALVES, columns // 2), BF16),
            pltpu.SemaphoreType.DMA((2 + 4 * N_DP,)),
            pltpu.SemaphoreType.DMA((3,)),
        ],
        compiler_params=pltpu.CompilerParams(vmem_limit_bytes=VMEM_LIMIT),
        cost_estimate=pl.CostEstimate(
            flops=10_000_000_000, bytes_accessed=20_000_000, transcendentals=745_472
        ),
    )(rows, gathered)


def result_kernel(hidden, gathered, out, units, full, rest, blocks, outs, sems, out_sems):
    unit_copies = [
        pltpu.make_async_copy(
            hidden.at[pl.ds(half * HALF, HALF), :],
            units.at[pl.ds(half * HALF, HALF), :],
            sems.at[2 * N_DP + half],
        )
        for half in range(2)
    ]
    copies, rest_copies = [], []
    for shard in range(N_DP):
        start = shard * SECOND_ROWS
        copies.append(
            pltpu.make_async_copy(
                gathered.at[pl.ds(start, SPLIT[1]), :],
                full.at[pl.ds(shard * SPLIT[1], SPLIT[1]), :],
                sems.at[2 * shard],
            )
        )
        rest_copies.append(
            pltpu.make_async_copy(
                gathered.at[pl.ds(start + SPLIT[1], SECOND_REST), :],
                blocks.at[shard],
                sems.at[2 * shard + 1],
            )
        )
    for copy in rest_copies + [unit_copies[0]] + copies + [unit_copies[1]]:
        copy.start()
    for copy in rest_copies:
        copy.wait()
    for shard in range(N_DP):
        for block in range(MAIN // 128):
            at = shard * SPLIT[1] + block * SECOND_REST
            middle = at + SPLIT[1] // 2
            both = blocks[shard, :, block * 128 : (block + 1) * 128]
            rest[at : at + SECOND_REST, :] = both[:, :REST]
            rest[middle : middle + SECOND_REST, :] = right_side(both)
    for copy in [unit_copies[0]] + copies:
        copy.wait()
    out_copies = []
    for half in range(2):
        if half == 1:
            unit_copies[1].wait()
        at = slice(half * HALF, (half + 1) * HALF)
        result = dot_t(units[at, :MAIN], full[...]) + dot_t(units[at, MAIN:], rest[...])
        close_rows(result, outs.at[half])
        copy = pltpu.make_async_copy(
            outs.at[half],
            out.at[pl.ds(half * HALF * HALVES, HALF * HALVES), :],
            out_sems.at[half],
        )
        copy.start()
        out_copies.append(copy)
    for copy in out_copies:
        copy.wait()


def results(hidden, gathered):
    columns = N_DP * SPLIT[1]
    hbm = pl.BlockSpec(memory_space=pltpu.HBM)
    return pl.pallas_call(
        result_kernel,
        out_shape=jax.ShapeDtypeStruct((EXPERTS * BLOCK, columns // 2), BF16),
        in_specs=[hbm, hbm],
        out_specs=hbm,
        scratch_shapes=[
            pltpu.VMEM((SLOTS, HID), BF16),
            pltpu.VMEM((columns, MAIN), BF16),
            pltpu.VMEM((columns, REST), BF16),
            pltpu.VMEM((N_DP, SECOND_REST, MAIN), BF16),
            pltpu.VMEM((2, HALF * HALVES, columns // 2), BF16),
            pltpu.SemaphoreType.DMA((2 * N_DP + 2,)),
            pltpu.SemaphoreType.DMA((2,)),
        ],
        compiler_params=pltpu.CompilerParams(vmem_limit_bytes=63 * 1024 * 1024),
        cost_estimate=pl.CostEstimate(
            flops=3_000_000_000, bytes_accessed=8_000_000, transcendentals=0
        ),
    )(hidden, gathered)


TERMS = 2
SHARE_ROWS = TERMS * ROWS


def share_kernel(ids, weights, total, out, repeated, slots, terms):
    at_group = pl.program_id(0)
    for copy in range(EXPERTS // 2 // GROUPS):
        repeated[copy] = total[...].astype(BF16)

    @pl.when(at_group == 0)
    def _():
        slots[...] = slot_table(ids).astype(BF16)
        shares = jnp.zeros((ROWS, EXPERTS), F32)
        for choice in range(TOP):
            named = ids[:, choice : choice + 1] == iota((ROWS, EXPERTS), 1)
            shares = shares + jnp.where(named, weights[:, choice : choice + 1], 0.0)
        high = shares.astype(BF16)
        terms[:ROWS, :] = high
        terms[ROWS:, :] = (shares - high.astype(F32)).astype(BF16)

    row = iota((EXPERTS, GROUP_ROWS), 1)
    pick = (over_56(row) + at_group * GROUP == iota((EXPERTS, GROUP_ROWS), 0)).astype(BF16)
    lane = iota((ROWS, GROUP_ROWS), 1)
    slot_of = lane - over_28(lane) * CAPACITY
    match = dot(slots[...], pick) == slot_of.astype(F32)
    shares = dot(terms[...], pick)
    for term in range(TERMS):
        at = slice(term * ROWS, (term + 1) * ROWS)
        out[at, :] = jnp.where(match, shares[at], 0.0).astype(BF16)


def share_table(ids, weights, total):
    chips = EXPERTS // 2
    return pl.pallas_call(
        share_kernel,
        grid=(GROUPS,),
        in_specs=[
            whole_block((ROWS, TOP)),
            whole_block((ROWS, TOP)),
            whole_block(total.shape),
        ],
        out_specs=(
            pl.BlockSpec((SHARE_ROWS, GROUP_ROWS), lambda i: (i, 0)),
            pl.BlockSpec((chips // GROUPS,) + total.shape, lambda i: (i, 0, 0)),
        ),
        out_shape=(
            jax.ShapeDtypeStruct((GROUPS * SHARE_ROWS, GROUP_ROWS), BF16),
            jax.ShapeDtypeStruct((chips,) + total.shape, BF16),
        ),
        scratch_shapes=[
            pltpu.VMEM((ROWS, EXPERTS), BF16),
            pltpu.VMEM((TERMS * ROWS, EXPERTS), BF16),
        ],
        compiler_params=pltpu.CompilerParams(vmem_limit_bytes=VMEM_LIMIT),
        cost_estimate=pl.CostEstimate(
            flops=50_000_000, bytes_accessed=3_000_000, transcendentals=0
        ),
    )(ids, weights, total)


def mix_blocks(shares, returned, table, blocks, total, sems, later=()):
    share_copies = [
        pltpu.make_async_copy(
            shares.at[pl.ds(g * SHARE_ROWS, SHARE_ROWS), :],
            table.at[pl.ds(g * SHARE_ROWS, SHARE_ROWS), :],
            sems.at[g],
        )
        for g in range(GROUPS)
    ]
    copies = [
        pltpu.make_async_copy(
            returned.at[pl.ds(g * GROUP_ROWS, GROUP_ROWS), :],
            blocks.at[pl.ds(g * GROUP_ROWS, GROUP_ROWS), :],
            sems.at[GROUPS + g],
        )
        for g in range(GROUPS)
    ]
    for g in range(GROUPS):
        share_copies[g].start()
        copies[g].start()
    for copy in later:
        copy.start()
    row = iota((1, GROUP_ROWS), 1)
    half_of = over_28(row) - over_56(row) * HALVES
    masks = [(half_of == half).astype(BF16) for half in range(HALVES)]
    for g in range(GROUPS):
        share_copies[g].wait()
        copies[g].wait()
        counts = table[g * SHARE_ROWS : (g + 1) * SHARE_ROWS, :]
        counts = jnp.concatenate([counts * mask for mask in masks], axis=0)
        found = dot(counts, blocks[g * GROUP_ROWS : (g + 1) * GROUP_ROWS, :])
        for half in range(HALVES):
            at = half * SHARE_ROWS
            part = found[at : at + ROWS] + found[at + ROWS : at + SHARE_ROWS]
            at = slice(half * ROWS, (half + 1) * ROWS)
            total[at, :] = part if g == 0 else total[at, :] + part
    for copy in later:
        copy.wait()


def mix_kernel(shares, returned, out, table, blocks, total, sems):
    mix_blocks(shares, returned, table, blocks, total, sems)
    width = returned.shape[1]
    out[:, :width] = total[:ROWS, :]
    out[:, width:] = total[ROWS:, :]


def last_kernel(
    shares, returned, first, latents, out, table, blocks, total, sems, others, own, last_sems
):
    copies = [
        pltpu.make_async_copy(first, others, last_sems.at[0]),
        pltpu.make_async_copy(latents, own, last_sems.at[1]),
    ]
    mix_blocks(shares, returned, table, blocks, total, sems, copies)
    pieces = []
    for shard in range(N_DP):
        half, at = shard // 4, shard % 4 * SPLIT[1]
        pieces.append(others[:, shard * SPLIT[0] : (shard + 1) * SPLIT[0]])
        pieces.append(total[half * ROWS : (half + 1) * ROWS, at : at + SPLIT[1]])
    whole = jnp.concatenate(pieces, axis=1)
    out[...] = (own[...].astype(F32) + whole).astype(BF16)


def mixed(shares, returned, *last):
    width = returned.shape[1]
    hbm = pl.BlockSpec(memory_space=pltpu.HBM)
    early = pl.BlockSpec(memory_space=pl.ANY) if last else hbm
    out, kernel = jax.ShapeDtypeStruct((ROWS, 2 * width), F32), mix_kernel
    scratch = [
        pltpu.VMEM(shares.shape, BF16),
        pltpu.VMEM(returned.shape, BF16),
        pltpu.VMEM((HALVES * ROWS, width), F32),
        pltpu.SemaphoreType.DMA((2 * GROUPS,)),
    ]
    if last:
        out, kernel = jax.ShapeDtypeStruct((ROWS, WIDTH), BF16), last_kernel
        scratch += [pltpu.VMEM(value.shape, value.dtype) for value in last]
        scratch += [pltpu.SemaphoreType.DMA((2,))]
    return pl.pallas_call(
        kernel,
        in_specs=[early, hbm] + [early] * len(last),
        out_shape=out,
        out_specs=pl.BlockSpec(memory_space=pltpu.VMEM),
        scratch_shapes=scratch,
        compiler_params=pltpu.CompilerParams(vmem_limit_bytes=(24 if last else 63) * 1024 * 1024),
        cost_estimate=pl.CostEstimate(
            flops=1_200_000_000, bytes_accessed=4_000_000, transcendentals=0
        ),
    )(shares, returned, *last)


SAME_CORE = [list(range(core, EXPERTS, 2)) for core in range(2)]


def other_core(value):
    return lax.ppermute(value, "expert", [(at, at ^ 1) for at in range(EXPERTS)])


def between_chips(pieces):
    return lax.all_to_all(
        pieces,
        "expert",
        split_axis=0,
        concat_axis=0,
        tiled=True,
        axis_index_groups=SAME_CORE,
    )


def scattered(part):
    pieces = between_chips(part.reshape(EXPERTS // 2, -1, WIDTH))
    return jnp.sum(pieces.astype(F32), axis=0)


def exchange_sum(total, bit):
    return total + lax.ppermute(total, "dp", [(at, at ^ bit) for at in range(N_DP)])


def both_halves(half):
    far_half = other_core(half)
    low = lax.axis_index("expert") % 2 == 0
    whole = jnp.concatenate(
        [jnp.where(low, half, far_half), jnp.where(low, far_half, half)], axis=0
    )
    return whole.astype(F32)


def exchanged(blocks):
    rows, columns = blocks.shape
    return lax.all_to_all(
        blocks.reshape(EXPERTS, rows // EXPERTS, columns),
        "expert",
        split_axis=0,
        concat_axis=0,
        tiled=True,
    ).reshape(rows, columns)


def tied(*values):
    return lax.optimization_barrier(values)


def per_device(
    queries,
    patch_keys,
    patch_values,
    norm_gain,
    gate_weight,
    up_weight,
    down_weight,
    expert_ids,
    combine_weights,
    latent_grad,
):
    parity = lax.axis_index("expert") % 2
    which = parity.reshape(1).astype(jnp.int32)
    far_keys, far_values = other_core(patch_keys), other_core(patch_values)
    shard, second_shard = packed(gate_weight[0], up_weight[0], down_weight[0].T)
    gathered = lax.all_gather(shard, "dp", axis=0, tiled=True)
    patches = (which, queries, patch_keys, far_keys, patch_values, far_values)
    latents, grad_part = attention(*patches, latent_grad)
    latents, second_shard = tied(latents, second_shard)
    second_gathered = lax.all_gather(second_shard, "dp", axis=0, tiled=True)
    total = scattered(grad_part)
    sent = dispatch(latents, norm_gain.reshape(1, WIDTH), expert_ids)
    sent, total, same_ids = tied(sent, total, expert_ids)
    received = exchanged(sent)
    total = exchange_sum(exchange_sum(exchange_sum(total, 1), 2), 4)
    shares, repeated = share_table(same_ids, combine_weights, total)
    received, repeated, shares = tied(received, repeated, shares)
    rows = opened(received)
    rows, repeated = tied(rows, repeated)
    half = between_chips(repeated).reshape(-1, WIDTH)
    hidden, first = experts(rows, gathered)
    hidden, first, half = tied(hidden, first, half)
    first = exchanged(first)
    second = exchanged(results(hidden, second_gathered))
    first_mix = mixed(shares, first)
    layer_out = mixed(shares, second, first_mix, latents)
    query_grad = both_halves(half)
    return (layer_out, query_grad)


def solution(mesh):
    return jax.shard_map(
        per_device,
        mesh=mesh,
        in_specs=(
            P(),
            P(("dp", "expert"), None),
            P(("dp", "expert"), None),
            P(),
            P("expert", "dp", None),
            P("expert", "dp", None),
            P("expert", None, "dp"),
            P(("dp", "expert"), None),
            P(("dp", "expert"), None),
            P(("dp", "expert"), None),
        ),
        out_specs=(P(("dp", "expert"), None), P()),
        check_vma=False,
    )
```
